256 devices in a mesh: st: 64 (over y, z, x_lo), head: 4 (over x_hi, core).
Axes of the slice: x: 4 (x_hi: 2, x_lo: 2; x = x_hi * 2 + x_lo), y: 4, z: 8, core: 2. Of those that a mesh axis runs over, the one named last changes fastest.
Arguments:
- video_tokens: bfloat16 [16384, 1536], P('st'), may hold values from -6 to 6
- cotangent: bfloat16 [16384, 1536], P('st'), may hold values from -6 to 6
- audio_frames: bfloat16 [8192, 1536], P('st'), may hold values from -6 to 6
- input_weights: bfloat16 [3, 1536, 1536], P(None, None, 'head'), may hold values from -0.15625 to 0.15625
- audio_weights: bfloat16 [2, 1536, 1536], P(None, None, 'head'), may hold values from -0.15625 to 0.15625
- output_weight: bfloat16 [1536, 1536], P('head'), may hold values from -0.75 to 0.75
- modulation: float32 [4, 3, 1536], replicated, may hold values from -3 to 3
- tile_clip: int32 [64], replicated, may hold values from 0 to 3, never falling along the last dimension, each value on 1 to 32 neighbouring positions
- dropped: int32 [4], replicated, may hold values 0 or 1
- audio_tile: int32 [8192, 1], P('st'), may hold values from 0 to 63; in each aligned block of 128 rows (0 to 127, 128 to 255, ...) at most 4 rows name the same one
Outputs:
- video_out: bfloat16 [16384, 1536], P('st', 'head')
- video_grad: bfloat16 [16384, 1536], P('st', 'head')
- audio_grad: bfloat16 [8192, 1536], P('st', 'head')
The draws below stay inside these ranges and needn't reach their ends.
Inputs may be any that keep to these rules, and one draw needn't show every extreme that they name: `tile_clip`: clip numbers never fall along the tiles; each clip spans 1 to 32 consecutive tiles, one exactly 32. `audio_tile`: among the 128 rows of one index of st no tile is named more than 4 times, a bound that some block reaches.
All inputs are finite; a program needn't handle non-finite values.
Results may differ from the reference program's by a relative error of at most 0.039.
Values may be sent and summed in bfloat16 or wider, within the bound.
No kernel may reach another device: no remote copies, remote signals or barrier semaphores. Data moves between devices by JAX's collectives and lax.ppermute only.
A program may use at most 64 MiB of HBM per device.

```python
import math
import jax
import jax.numpy as jnp
import numpy as np
from jax import lax

D = 1536
HD = 64
TOK_DEV = 256
TILES = 64
TOKENS = 16384
AUD_DEV = 128
AUDIO = 8192
CAP = 4
CLIPS = 4
CLIP_TILES = 32
N_ST = 64
N_HEAD = 4


def touch_ends(values, own_key, low, top_value):
    longest = values.shape.index(max(values.shape))
    spots = []
    for shift in (0, 1):
        where = [jax.random.randint(jax.random.fold_in(own_key, axis), (), 0, length) for axis, length in enumerate(values.shape)]
        where[longest] = (where[longest] + shift) % values.shape[longest]
        spots.append(tuple(where))
    return values.at[spots[0]].set(low).at[spots[1]].set(top_value)


def steps_of(key, dims, cuts, low, top_value):
    factor_of = 1.0
    for dim, parts in cuts:
        heights = jax.random.uniform(jax.random.fold_in(jax.random.fold_in(key, 6), dim), (parts,), jnp.float32, low / len(cuts), top_value / len(cuts))
        factor_of = factor_of * jnp.repeat(jnp.exp(heights), dims[dim] // parts).reshape((-1,) + (1,) * (len(dims) - 1 - dim))
    return factor_of


def length_profile(count, total, limit, skew):
    loads = [(1 << 20) // math.isqrt(standing ** skew) + 1 for standing in range(2, count + 1)]
    spare, given = total - limit - (count - 1), [1] * (count - 1)
    while spare > 0:
        free = [i for i in range(count - 1) if given[i] < limit]
        pool, remaining = sum([loads[i] for i in free]), spare
        for i in free:
            extra = min(limit - given[i], max(1, remaining * loads[i] // pool), spare)
            given[i] = given[i] + extra
            spare = spare - extra
    return np.array([limit] + given)


def uneven(stream_key, number_of, total, reach, lean):
    if number_of == 2:
        one = jax.random.randint(stream_key, (), max(1, total - reach), min(reach, total - 1) + 1)
        return jnp.stack([one, total - one])
    sizes = jnp.asarray(length_profile(number_of, total, reach, lean), jnp.int32)
    twos = (number_of - 1) // 2
    source_of, taker = sizes[1:1 + 2 * twos:2], sizes[2:2 + 2 * twos:2]
    slack = jnp.minimum(source_of - 1, reach - taker)
    passed = jax.random.randint(jax.random.fold_in(stream_key, 1), (twos,), 0, 1 << 20) % (slack + 1)
    sizes = sizes.at[1:1 + 2 * twos:2].set(source_of - passed).at[2:2 + 2 * twos:2].set(taker + passed)
    return sizes[jax.random.permutation(jax.random.fold_in(stream_key, 2), number_of)]


def routed_block(key, own, number, rows, count, top, reach, lean):
    order = jax.random.permutation(key, count)
    packed, ordinary = shares(count, rows * top, reach, lean, True), shares(count, rows * top, reach, lean, False)
    places = jnp.arange(count)

    def named(lengths, rotation):
        used = int((lengths > 0).sum())
        fixed = max(1, used // 4)
        passed = fixed + (places - fixed + rotation * (used - fixed)) % max(1, count - fixed)
        return jnp.zeros((count,), jnp.int32).at[order[jnp.where(places < fixed, places, passed)]].set(jnp.asarray(lengths, jnp.int32))

    lengths = jnp.where(number % 4 == 0, named(packed, number // 4), named(ordinary, number - number // 4 - 1))
    mixed = jax.random.permutation(jax.random.fold_in(own, 3), count)
    donor, sink = mixed[0:count // 2 * 2:2], mixed[1:count // 2 * 2:2]
    slack = jnp.minimum(lengths[donor] - 1, reach - lengths[sink]) // 2
    slack = jnp.where((donor == order[0]) | (sink == order[0]) | (lengths[sink] == 0), 0, jnp.maximum(slack, 0))
    passed = jax.random.randint(jax.random.fold_in(own, 4), (count // 2,), 0, 1 << 20) % (slack + 1)
    lengths = lengths.at[donor].add(-passed).at[sink].add(passed)
    items = jnp.searchsorted(jnp.cumsum(lengths), jnp.arange(rows * top), side="right").astype(jnp.int32)
    listing = items.reshape(top, rows).T
    listing = listing[jax.random.permutation(jax.random.fold_in(own, 1), rows)]
    rotation = jax.random.randint(jax.random.fold_in(own, 2), (rows, 1), 0, top)
    return jnp.take_along_axis(listing, (jnp.arange(top)[None, :] + rotation) % top, axis=1)


def shares(count, total, reach, skew, full):
    weights = [(1 << 20) // math.isqrt(rank ** skew) + 1 for rank in range(1, count + 1)]
    largest = reach if full else min(reach, max(-(-total // count), total * weights[0] // sum(weights)))
    least = 1 if total - largest >= count - 1 else 0
    holding, spare = [largest] + [least] * (count - 1), total - largest - least * (count - 1)
    while spare > 0:
        candidates = [i for i in range(1, count) if holding[i] < largest] or [i for i in range(1, count) if holding[i] < reach]
        pool, left = sum([weights[i] for i in candidates]), spare
        for i in candidates:
            more = min(reach - holding[i], max(1, left * weights[i] // pool), spare)
            holding[i] = holding[i] + more
            spare = spare - more
    return np.array(holding)


def noise(rng, extent, deviation, most, split=(), kind=jnp.bfloat16):
    loudness = steps_of(rng, extent, split, -0.22, 0.18) if split else 1.0
    drawn = jax.random.normal(rng, extent, jnp.float32) * deviation * loudness
    return jnp.minimum(jnp.maximum(drawn, -most), most).astype(kind)


def setup_inputs(seed: int = 0) -> dict:
    key_of = jax.random.split(jax.random.key(seed), 11)
    video_tokens = noise(key_of[0], (TOKENS, D), 1.0, 6.0, ((0, 64),))
    cotangent = noise(key_of[1], (TOKENS, D), 1.0, 6.0, ((0, 64),))
    audio_frames = noise(key_of[2], (AUDIO, D), 1.0, 6.0, ((0, 64),))
    input_weights = noise(key_of[3], (3, D, D), D ** -0.5, 0.15625, ((2, 4),))
    audio_weights = noise(key_of[4], (2, D, D), D ** -0.5, 0.15625, ((2, 4),))
    output_weight = noise(key_of[5], (D, D), HD ** -0.5, 0.75, ((0, 4),))
    modulation = noise(key_of[6], (CLIPS, 3, D), 1.0, 3.0, (), jnp.float32)
    tile_clip = jnp.searchsorted(jnp.cumsum(uneven(key_of[7], CLIPS, TILES, CLIP_TILES, 0)), jnp.arange(TILES), side="right").astype(jnp.int32)
    dropped = touch_ends((jax.random.randint(key_of[8], (CLIPS,), 0, 4) < 1).astype(jnp.int32), jax.random.fold_in(key_of[8], 1), 0, 1)
    audio_tile_keys = jax.random.split(jax.random.fold_in(key_of[9], 1), AUDIO // AUD_DEV)
    audio_tile_turns = jax.random.permutation(jax.random.fold_in(key_of[9], 3), AUDIO // AUD_DEV)
    audio_tile = jax.vmap(lambda own, number: routed_block(jax.random.fold_in(key_of[9], 2), own, number, AUD_DEV, TILES, 1, CAP, 2))(audio_tile_keys, audio_tile_turns).reshape((AUDIO, 1))
    return {"video_tokens": video_tokens, "cotangent": cotangent, "audio_frames": audio_frames, "input_weights": input_weights, "audio_weights": audio_weights, "output_weight": output_weight, "modulation": modulation, "tile_clip": tile_clip, "dropped": dropped, "audio_tile": audio_tile}


epsilon = 1e-06

def row_scale(matrix):
    return lax.rsqrt(lax.optimization_barrier(jnp.mean(matrix * matrix, axis=-1, keepdims=True)) + epsilon)

def weights_for(queries, key_rows, key_mask):
    factor = float(HD) ** (-0.5)
    scores = jnp.einsum('nhe,mhe->hnm', queries.astype(jnp.float32), key_rows[:, 0].astype(jnp.float32)) * factor
    weights = jnp.exp(scores) * key_mask[None, None, :]
    totals = lax.optimization_barrier(jnp.sum(weights, axis=-1))
    return weights / totals[:, :, None]

def to_bf_and_back(matrix):
    return lax.optimization_barrier(matrix.astype(jnp.bfloat16)).astype(jnp.float32)

def reference(video_tokens, cotangent, audio_frames, input_weights, audio_weights, output_weight, modulation, tile_clip, dropped, audio_tile):
    head_count = D // HD
    group_width = D // N_HEAD
    factor = float(HD) ** (-0.5)
    tile_mods = modulation[tile_clip]
    shifts = tile_mods[:, 0][:, None, :]
    scales = tile_mods[:, 1][:, None, :]
    gating = tile_mods[:, 2][:, None, :]
    inputs = video_tokens.astype(jnp.float32).reshape(N_ST, TOK_DEV, D)
    input_scale = row_scale(inputs)
    normed = inputs * input_scale
    modulated = (normed * (1.0 + scales) + shifts).astype(jnp.bfloat16).reshape(TOKENS, D)
    query_flat = jnp.dot(modulated, input_weights[0], preferred_element_type=jnp.float32).astype(jnp.bfloat16)
    key_flat = jnp.dot(modulated, input_weights[1], preferred_element_type=jnp.float32).astype(jnp.bfloat16)
    value_flat = jnp.dot(modulated, input_weights[2], preferred_element_type=jnp.float32).astype(jnp.bfloat16)
    query_tiles = query_flat.reshape(N_ST, TOK_DEV, head_count, HD)
    pair_tiles = jnp.stack((key_flat, value_flat), axis=1).reshape(N_ST, TOK_DEV, 2, head_count, HD)
    sounds = audio_frames.astype(jnp.float32)
    sound_scale = row_scale(sounds)
    sound_normed = sounds * sound_scale
    sound_in = sound_normed.astype(jnp.bfloat16)
    sound_keys = jnp.dot(sound_in, audio_weights[0], preferred_element_type=jnp.float32).astype(jnp.bfloat16)
    sound_values = jnp.dot(sound_in, audio_weights[1], preferred_element_type=jnp.float32).astype(jnp.bfloat16)
    sound_pairs = jnp.stack((sound_keys, sound_values), axis=1).reshape(AUDIO, 2, head_count, HD)
    targets = audio_tile[:, 0].reshape(N_ST, AUD_DEV)
    tile_ids = jnp.arange(N_ST, dtype=jnp.int32)
    target_hot = (targets[:, :, None] == tile_ids[None, None, :]).astype(jnp.int32)
    slot_rank = jnp.cumsum(target_hot, axis=1) - 1
    alive_rows = 1 - dropped[tile_clip[targets]]
    depth_ids = jnp.arange(CAP, dtype=jnp.int32)
    slot_hits = target_hot[:, :, :, None] * (slot_rank[:, :, :, None] == depth_ids[None, None, None, :]).astype(jnp.int32) * alive_rows[:, :, None, None]
    local_ids = jnp.arange(AUD_DEV, dtype=jnp.int32)
    row_of = lax.optimization_barrier(jnp.sum(slot_hits * local_ids[None, :, None, None], axis=1)) + (tile_ids * AUD_DEV)[:, None, None]
    filled = lax.optimization_barrier(jnp.sum(slot_hits, axis=1))
    slot_rows = jnp.transpose(row_of, (1, 0, 2)).reshape(N_ST, N_ST * CAP)
    slot_live = jnp.transpose(filled, (1, 0, 2)).reshape(N_ST, N_ST * CAP).astype(jnp.float32)
    same_next = (tile_clip[1:] == tile_clip[:-1]).astype(jnp.float32)
    zero_one = jnp.zeros((1,), jnp.float32)
    left_ok = jnp.concatenate((zero_one, same_next))
    right_ok = jnp.concatenate((same_next, zero_one))

    def keys_for(tile_index):
        before = pair_tiles[jnp.maximum(tile_index - 1, 0)]
        following = pair_tiles[jnp.minimum(tile_index + 1, N_ST - 1)]
        slot_pairs = sound_pairs[slot_rows[tile_index]]
        key_rows = jnp.concatenate((before, pair_tiles[tile_index], following, slot_pairs), axis=0)
        edge_ones = jnp.ones((TOK_DEV,), jnp.float32)
        key_mask = jnp.concatenate((edge_ones * left_ok[tile_index], edge_ones, edge_ones * right_ok[tile_index], slot_live[tile_index]))
        return (key_rows, key_mask)

    def forward_tile(tile_index):
        key_rows, key_mask = keys_for(tile_index)
        rounded = weights_for(query_tiles[tile_index], key_rows, key_mask).astype(jnp.bfloat16)
        return jnp.einsum('hnm,mhe->nhe', rounded.astype(jnp.float32), key_rows[:, 1].astype(jnp.float32)).astype(jnp.bfloat16)
    attended = lax.map(forward_tile, tile_ids).reshape(TOKENS, D)
    out_sum = jnp.zeros((TOKENS, D), jnp.float32)
    for head_group in range(N_HEAD):
        first_col = head_group * group_width
        term = jnp.dot(attended[:, first_col:first_col + group_width], output_weight[first_col:first_col + group_width], preferred_element_type=jnp.float32)
        out_sum = out_sum + to_bf_and_back(term)
    video_out = (inputs + gating * out_sum.reshape(N_ST, TOK_DEV, D)).astype(jnp.bfloat16).reshape(TOKENS, D)
    out_grad = (cotangent.astype(jnp.float32).reshape(N_ST, TOK_DEV, D) * gating).astype(jnp.bfloat16).reshape(TOKENS, D)
    attended_grad = jnp.dot(out_grad, output_weight.T, preferred_element_type=jnp.float32).astype(jnp.bfloat16)
    grad_tiles = attended_grad.reshape(N_ST, TOK_DEV, head_count, HD)
    attended_tiles = attended.reshape(N_ST, TOK_DEV, head_count, HD)

    def backward_tile(carried, tile_index):
        pending, incoming = carried
        key_rows, key_mask = keys_for(tile_index)
        queries = query_tiles[tile_index].astype(jnp.float32)
        output_grad = grad_tiles[tile_index].astype(jnp.float32)
        row_dots = jnp.einsum('nhe,nhe->hn', output_grad, attended_tiles[tile_index].astype(jnp.float32))
        probabilities = weights_for(query_tiles[tile_index], key_rows, key_mask)
        rounded = probabilities.astype(jnp.bfloat16).astype(jnp.float32)
        weight_grad = jnp.einsum('nhe,mhe->hnm', output_grad, key_rows[:, 1].astype(jnp.float32))
        score_grad = to_bf_and_back(probabilities * (weight_grad - row_dots[:, :, None]))
        query_grad = jnp.einsum('hnm,mhe->nhe', score_grad, key_rows[:, 0].astype(jnp.float32)) * factor
        key_grad = jnp.einsum('hnm,nhe->mhe', score_grad, queries) * factor
        value_grad = jnp.einsum('hnm,nhe->mhe', rounded, output_grad)
        all_grad = jnp.stack((key_grad, value_grad), axis=1)
        finished = pending + all_grad[:TOK_DEV]
        carried_next = (all_grad[TOK_DEV:2 * TOK_DEV] + incoming, all_grad[2 * TOK_DEV:3 * TOK_DEV])
        return (carried_next, (finished.astype(jnp.bfloat16), query_grad.astype(jnp.bfloat16), all_grad[3 * TOK_DEV:].astype(jnp.bfloat16)))
    zero_tile = jnp.zeros((TOK_DEV, 2, head_count, HD), jnp.float32)
    (last_tile, leftover), (finished, query_grads, slot_grads) = lax.scan(backward_tile, (zero_tile, zero_tile), tile_ids)
    pair_grads = jnp.concatenate((finished[1:], last_tile.astype(jnp.bfloat16)[None]), axis=0)
    query_all = query_grads.reshape(TOKENS, D)
    pair_flat = pair_grads.reshape(TOKENS, 2, D)
    slot_flat = slot_grads.reshape(N_ST * N_ST * CAP, 2, D).astype(jnp.float32) * slot_live.reshape(-1)[:, None, None]
    sound_grad = jnp.zeros((AUDIO, 2, D), jnp.float32).at[slot_rows.reshape(-1)].add(slot_flat).astype(jnp.bfloat16)
    video_sum = jnp.zeros((TOKENS, D), jnp.float32)
    sound_sum = jnp.zeros((AUDIO, D), jnp.float32)
    for head_group in range(N_HEAD):
        first_col = head_group * group_width
        last_col = first_col + group_width
        video_term = jnp.dot(query_all[:, first_col:last_col], input_weights[0][:, first_col:last_col].T, preferred_element_type=jnp.float32)
        video_term = video_term + jnp.dot(pair_flat[:, 0, first_col:last_col], input_weights[1][:, first_col:last_col].T, preferred_element_type=jnp.float32)
        video_term = video_term + jnp.dot(pair_flat[:, 1, first_col:last_col], input_weights[2][:, first_col:last_col].T, preferred_element_type=jnp.float32)
        video_sum = video_sum + to_bf_and_back(video_term)
        sound_term = jnp.dot(sound_grad[:, 0, first_col:last_col], audio_weights[0][:, first_col:last_col].T, preferred_element_type=jnp.float32)
        sound_term = sound_term + jnp.dot(sound_grad[:, 1, first_col:last_col], audio_weights[1][:, first_col:last_col].T, preferred_element_type=jnp.float32)
        sound_sum = sound_sum + to_bf_and_back(sound_term)
    hat_grad = video_sum.reshape(N_ST, TOK_DEV, D) * (1.0 + scales)
    video_grad = cotangent.astype(jnp.float32).reshape(N_ST, TOK_DEV, D) + input_scale * (hat_grad - normed * lax.optimization_barrier(jnp.mean(hat_grad * normed, axis=-1, keepdims=True)))
    audio_grad = sound_scale * (sound_sum - sound_normed * lax.optimization_barrier(jnp.mean(sound_sum * sound_normed, axis=-1, keepdims=True)))
    return (video_out, video_grad.astype(jnp.bfloat16).reshape(TOKENS, D), audio_grad.astype(jnp.bfloat16))
```

```python
import jax
import jax.numpy as jnp
from jax import lax
from jax.experimental import pallas as pl
from jax.experimental.pallas import tpu as pltpu
from jax.sharding import PartitionSpec as P

HD = 64
EPS = 1e-06
DEAD = -1e30
EMPTY = 32768.0
LOG4 = 1.3862943611198906
F32 = jnp.float32
BF16 = jnp.bfloat16
VMEM_LIMIT = 56 * 1024 * 1024

NN = (((1,), (0,)), ((), ()))
NT = (((1,), (1,)), ((), ()))
TN = (((0,), (0,)), ((), ()))


def mm(a, b, dims=NN):
    return lax.dot_general(a, b, dims, preferred_element_type=F32)


def iota(shape, dim):
    return lax.broadcasted_iota(jnp.int32, shape, dim)


def row_scale(matrix):
    return lax.rsqrt(jnp.mean(matrix * matrix, axis=-1, keepdims=True) + EPS)


def to_row(col):
    n = col.shape[0]
    eye = iota((n, n), 0) == iota((n, n), 1)
    return jnp.sum(jnp.where(eye, col, jnp.zeros_like(col)), axis=0, keepdims=True)


def to_col(row):
    n = row.shape[1]
    eye = iota((n, n), 0) == iota((n, n), 1)
    return jnp.sum(jnp.where(eye, row, jnp.zeros_like(row)), axis=1, keepdims=True)


def fetch(pairs, sems):
    copies = [pltpu.make_async_copy(src, dst, sems.at[i]) for i, (src, dst) in enumerate(pairs)]
    for copy in copies:
        copy.start()
    return copies


def audio_front(audio_ref, target_ref, weights_hbm, out_ref, weights, sems):
    rows = audio_ref.shape[0]
    copies = fetch([(weights_hbm.at[i], weights.at[i]) for i in range(2)], sems)
    sounds = audio_ref[...].astype(F32)
    sound_in = (sounds * row_scale(sounds)).astype(BF16)
    tcol = target_ref[...]
    trow = to_row(tcol)
    earlier = (tcol == trow) & (iota((rows, rows), 0) < iota((rows, rows), 1))
    rank = jnp.sum(earlier.astype(jnp.int32), axis=0, keepdims=True)
    slot = trow * 8 + rank
    slots = out_ref.shape[0]
    place = iota((slots, rows), 0)
    to_key = (place == slot).astype(BF16)
    to_value = (place == slot + 4).astype(BF16)
    dispatch = jnp.concatenate((to_key, to_value), axis=1)
    filled = jnp.sum(dispatch.astype(F32), axis=1, keepdims=True)
    pairs = []
    for i in range(2):
        copies[i].wait()
        pairs.append(mm(sound_in, weights[i]).astype(BF16))
    sent = mm(dispatch, jnp.concatenate(pairs, axis=0))
    shape = sent.shape
    mark = ((iota(shape, 0) & 7) < 4) & (iota(shape, 1) == 0) & (filled < 0.5)
    out_ref[...] = jnp.where(mark, EMPTY, sent).astype(BF16)


def video_front(tokens_ref, mod_ref, clip_ref, weights_hbm, kv_ref, modulated_ref, weights, sems):
    rows = tokens_ref.shape[0]
    copies = fetch([(weights_hbm.at[i + 1], weights.at[i]) for i in range(2)], sems)
    mod = mod_ref[clip_ref[lax.axis_index("st")]]
    inputs = tokens_ref[...].astype(F32)
    modulated = (inputs * row_scale(inputs) * (1.0 + mod[1:2]) + mod[0:1]).astype(BF16)
    modulated_ref[...] = modulated
    for i in range(2):
        copies[i].wait()
        kv_ref[pl.ds(i * rows, rows), :] = mm(modulated, weights[i]).astype(BF16)


def query_front(
    modulated_ref, cotangent_ref, mod_ref, clip_ref, wq_hbm, wo_hbm, q_ref, g_ref, gt_ref, wq, wo, sems
):
    copies = fetch([(wq_hbm.at[0], wq), (wo_hbm, wo)], sems)
    gating = mod_ref[clip_ref[lax.axis_index("st")]][2:3]
    out_grad = (cotangent_ref[...].astype(F32) * gating).astype(BF16)
    copies[0].wait()
    queries = mm(modulated_ref[...], wq[...]).astype(BF16)
    q_ref[...] = (queries.astype(F32) * (float(HD) ** -0.5)).astype(BF16)
    copies[1].wait()
    grads = mm(out_grad, wo[...], NT)
    g_ref[...] = grads.astype(BF16)
    gt_ref[...] = grads.T.astype(BF16)


def attention(
    clip_ref,
    dropped_ref,
    q_ref,
    g_ref,
    gt_ref,
    own_ref,
    left_ref,
    right_ref,
    slots_ref,
    at_ref,
    dq_ref,
    dl_ref,
    do_ref,
    dr_ref,
    ds_ref,
    aud_ref,
    daud_ref,
    bias_ref,
):
    rows, width = q_ref.shape
    slots = slots_ref.shape[0]
    half = slots // 2
    position = lax.axis_index("st")
    count = clip_ref.shape[0]
    clip = clip_ref[position]
    before = clip_ref[jnp.maximum(position - 1, 0)]
    after = clip_ref[jnp.minimum(position + 1, count - 1)]
    left_bias = jnp.where((before == clip) & (position > 0), -LOG4, DEAD)
    right_bias = jnp.where((after == clip) & (position < count - 1), -LOG4, DEAD)
    alive = dropped_ref[clip] == 0
    pick_row = iota((half, slots), 0)
    pick_at = (pick_row >> 2) * 8 + (pick_row & 3)
    arrived = slots_ref[...]
    for i in range(2):
        pick = (iota((half, slots), 1) == pick_at + 4 * i).astype(BF16)
        aud_ref[pl.ds(i * half, half), :] = mm(pick, arrived).astype(BF16)
    head = aud_ref[pl.ds(0, half), pl.ds(0, 128)].astype(F32)
    live = (head[:, 0:1] < EMPTY * 0.5) & alive
    bias_ref[...] = jnp.broadcast_to(jnp.where(live, -LOG4, DEAD), bias_ref.shape)
    lane = iota((rows, 128), 1)

    def pair_step(pair, carried):
        cols = pl.ds(pl.multiple_of(pair * 128, 128), 128)
        q_pair = q_ref[:, cols]
        g_pair = g_ref[:, cols]
        sources = (left_ref, own_ref, right_ref, aud_ref)
        keys = [ref[pl.ds(0, rows), cols] for ref in sources]
        values = [ref[pl.ds(rows, rows), cols] for ref in sources]
        keys_t = [k.T for k in keys]
        values_t = [v.T for v in values]
        d_keys = [jnp.zeros((rows, 128), F32) for _ in sources]
        d_values = [jnp.zeros((rows, 128), F32) for _ in sources]
        for side in range(2):
            mine = (lane // HD) == side
            q = jnp.where(mine, q_pair, jnp.zeros_like(q_pair))
            g = jnp.where(mine, g_pair, jnp.zeros_like(g_pair))
            head_rows = pl.ds(pl.multiple_of(pair * 128 + side * HD, HD), HD)
            biases = (left_bias, -LOG4, right_bias, jnp.concatenate([bias_ref[...]] * 2, axis=1))
            weights = [jnp.exp(mm(k, q, NT) + b) for k, b in zip(keys, biases)]
            totals = sum(jnp.sum(w, axis=0, keepdims=True) for w in weights)
            inverse = 1.0 / totals
            probs = [w * inverse for w in weights]
            rounded = [p.astype(BF16) for p in probs]
            att = sum(mm(v, p) for v, p in zip(values_t, rounded))
            att = att[side * HD : (side + 1) * HD].astype(BF16)
            at_ref[head_rows, :] = att
            dots = jnp.sum(att.astype(F32) * gt_ref[head_rows, :].astype(F32), axis=0, keepdims=True)
            score_grads = [
                (p * (mm(v, g, NT) - dots)).astype(BF16) for p, v in zip(probs, values)
            ]
            dq = sum(mm(k, s) for k, s in zip(keys_t, score_grads))
            dq = dq[side * HD : (side + 1) * HD] * (float(HD) ** -0.5)
            dq_ref[head_rows, :] = dq.astype(BF16)
            for b in range(4):
                d_keys[b] = d_keys[b] + mm(score_grads[b], q)
                d_values[b] = d_values[b] + mm(rounded[b], g)
        for b, ref in enumerate((dl_ref, do_ref, dr_ref, daud_ref)):
            ref[pl.ds(0, rows), cols] = d_keys[b].astype(ref.dtype)
            ref[pl.ds(rows, rows), cols] = d_values[b].astype(ref.dtype)
        return carried

    lax.fori_loop(0, width // 128, pair_step, 0)
    back_row = iota((slots, half), 0)
    back_at = (back_row >> 3) * 4 + (back_row & 3)
    total = jnp.zeros((slots, width), F32)
    for i in range(2):
        inside = (back_row & 4) == 4 * i
        put = ((iota((slots, half), 1) == back_at) & inside).astype(BF16)
        total = total + mm(put, daud_ref[pl.ds(i * half, half), :])
    ds_ref[...] = total.astype(BF16)


def out_project(at_ref, wo_ref, *out_refs):
    rows = at_ref.shape[0]
    attended = at_ref[...].astype(F32).T.astype(BF16)
    me = lax.axis_index("head")
    for k, ref in enumerate(out_refs):
        cols = pl.ds(pl.multiple_of((me ^ k) * rows, 128), rows)
        ref[...] = mm(attended, wo_ref[:, cols]).astype(BF16)


def input_project(
    dq_ref,
    do_ref,
    fl_ref,
    fr_ref,
    back_ref,
    tokens_ref,
    audio_ref,
    target_ref,
    mod_ref,
    clip_ref,
    weights_hbm,
    audio_weights_hbm,
    out0,
    out1,
    out2,
    out3,
    weights,
    audio_weights,
    sems,
):
    rows = tokens_ref.shape[0]
    sound_rows = audio_ref.shape[0]
    width = do_ref.shape[1]
    copies = fetch([(weights_hbm, weights), (audio_weights_hbm, audio_weights)], sems)
    me = lax.axis_index("head")
    mod = mod_ref[clip_ref[lax.axis_index("st")]]
    inputs = tokens_ref[...].astype(F32)
    normed = inputs * row_scale(inputs)
    sounds = audio_ref[...].astype(F32)
    sound_normed = sounds * row_scale(sounds)
    queries = dq_ref[...].astype(F32).T.astype(BF16)
    pair = do_ref[...] + fl_ref[...].astype(F32) + fr_ref[...].astype(F32)
    pair = pair.astype(BF16)
    tcol = target_ref[...]
    trow = to_row(tcol)
    earlier = (tcol == trow) & (iota((sound_rows, sound_rows), 1) < iota((sound_rows, sound_rows), 0))
    slot = tcol * 8 + jnp.sum(earlier.astype(jnp.int32), axis=1, keepdims=True)
    slots = back_ref.shape[0]
    back = back_ref[...]
    sound_grads = []
    for i in range(2):
        pick = (iota((sound_rows, slots), 1) == slot + 4 * i).astype(BF16)
        sound_grads.append(mm(pick, back).astype(BF16))
    for copy in copies:
        copy.wait()
    outs = (out0, out1, out2, out3)
    dots = jnp.zeros((rows, 1), F32)
    sound_dots = jnp.zeros((sound_rows, 1), F32)
    hat = normed * (1.0 + mod[1:2])
    for k in range(4):
        start = pl.multiple_of((me ^ k) * width, 128)
        feats = pl.ds(start, width)
        part = mm(queries, weights[0, feats, :], NT)
        part = part + mm(pair[:rows], weights[1, feats, :], NT)
        part = part + mm(pair[rows:], weights[2, feats, :], NT)
        sound_part = mm(sound_grads[0], audio_weights[0, feats, :], NT)
        sound_part = sound_part + mm(sound_grads[1], audio_weights[1, feats, :], NT)
        outs[k][pl.ds(0, rows), :] = part.astype(BF16)
        outs[k][pl.ds(rows, sound_rows), :] = sound_part.astype(BF16)
    for k in range(4):
        block = slice(k * width, (k + 1) * width)
        chunk = jnp.zeros((rows + sound_rows, width), F32)
        for j in range(4):
            chosen = (me ^ j) == k
            chunk = chunk + jnp.where(chosen, outs[j][pl.ds(0, rows + sound_rows), :].astype(F32), 0.0)
        dots = dots + jnp.sum(chunk[:rows] * hat[:, block], axis=1, keepdims=True)
        sound_dots = sound_dots + jnp.sum(
            chunk[rows:] * sound_normed[:, block], axis=1, keepdims=True
        )
    row = jnp.concatenate((to_row(dots), to_row(sound_dots)), axis=1)
    high = row.astype(BF16).astype(F32)
    low = row - high
    where_row = iota((16, rows + sound_rows), 0)
    extra = jnp.where(where_row == 0, high, jnp.where(where_row == 1, low, 0.0)).astype(BF16)
    for k in range(4):
        outs[k][pl.ds(rows + sound_rows, 16), :] = extra


def finish(
    tokens_ref,
    cotangent_ref,
    audio_ref,
    mod_ref,
    clip_ref,
    o0,
    o1,
    o2,
    o3,
    g0,
    g1,
    g2,
    g3,
    video_out_ref,
    video_grad_ref,
    audio_grad_ref,
):
    rows, width = video_out_ref.shape
    sound_rows = audio_grad_ref.shape[0]
    model = tokens_ref.shape[1]
    me = lax.axis_index("head")
    cols = pl.ds(pl.multiple_of(me * width, 128), width)
    clip = clip_ref[lax.axis_index("st")]
    mod = mod_ref[clip, :, cols]
    inputs = tokens_ref[...].astype(F32)
    scale = row_scale(inputs)
    mine = tokens_ref[:, cols].astype(F32)
    out_sum = sum(ref[...].astype(F32) for ref in (o0, o1, o2, o3))
    video_out_ref[...] = (mine + mod[2:3] * out_sum).astype(BF16)
    parts = (g0, g1, g2, g3)
    total = sum(ref[pl.ds(0, rows + sound_rows), :].astype(F32) for ref in parts)
    extra = sum(ref[pl.ds(rows + sound_rows, 16), :].astype(F32) for ref in parts)
    row = (extra[0:1] + extra[1:2]) * (1.0 / model)
    mean = to_col(row[:, :rows])
    sound_mean = to_col(row[:, rows:])
    hat = total[:rows] * (1.0 + mod[1:2])
    video_grad_ref[...] = (
        cotangent_ref[:, cols].astype(F32) + scale * (hat - mine * scale * mean)
    ).astype(BF16)
    sounds = audio_ref[...].astype(F32)
    sound_scale = row_scale(sounds)
    sound_mine = audio_ref[:, cols].astype(F32) * sound_scale
    audio_grad_ref[...] = (sound_scale * (total[rows:] - sound_mine * sound_mean)).astype(BF16)


VM = pl.BlockSpec(memory_space=pltpu.VMEM)
SM = pl.BlockSpec(memory_space=pltpu.SMEM)
HBM = pl.BlockSpec(memory_space=pl.ANY)


def call(body, ins, outs, flops, name, scratch=()):
    return pl.pallas_call(
        body,
        in_specs=list(ins),
        out_specs=[VM] * len(outs),
        out_shape=[jax.ShapeDtypeStruct(shape, dtype) for shape, dtype in outs],
        scratch_shapes=list(scratch),
        compiler_params=pltpu.CompilerParams(vmem_limit_bytes=VMEM_LIMIT),
        cost_estimate=pl.CostEstimate(flops=flops, bytes_accessed=4 << 20, transcendentals=0),
        name=name,
    )


def per_device(
    video_tokens,
    cotangent,
    audio_frames,
    input_weights,
    audio_weights,
    output_weight,
    modulation,
    tile_clip,
    dropped,
    audio_tile,
):
    rows, model = video_tokens.shape
    width = input_weights.shape[2]
    sound_rows = audio_frames.shape[0]
    count = lax.axis_size("st")
    slots = 8 * count
    dma = pltpu.SemaphoreType.DMA((2,))
    wide = pltpu.VMEM((2, model, width), BF16)
    (sent,) = call(
        audio_front,
        (VM, VM, HBM),
        [((slots, width), BF16)],
        2 * sound_rows * model * 2 * width,
        "audio_front",
        (wide, dma),
    )(audio_frames, audio_tile, audio_weights)
    arrived = lax.all_to_all(sent, "st", split_axis=0, concat_axis=0, tiled=True)
    kv, modulated = call(
        video_front,
        (VM, VM, SM, HBM),
        [((2 * rows, width), BF16), ((rows, model), BF16)],
        2 * rows * model * 2 * width,
        "video_front",
        (wide, dma),
    )(video_tokens, modulation, tile_clip, input_weights)
    up = [(i, i + 1) for i in range(count - 1)]
    down = [(i + 1, i) for i in range(count - 1)]
    from_left = lax.ppermute(kv, "st", up)
    from_right = lax.ppermute(kv, "st", down)
    queries, grads, grads_t = call(
        query_front,
        (VM, VM, VM, SM, HBM, HBM),
        [((rows, width), BF16), ((rows, width), BF16), ((width, rows), BF16)],
        2 * rows * model * 2 * width,
        "query_front",
        (pltpu.VMEM((model, width), BF16), pltpu.VMEM((width, model), BF16), dma),
    )(modulated, cotangent, modulation, tile_clip, input_weights, output_weight)
    half = slots // 2
    attended_t, dq_t, d_left, d_own, d_right, d_slots = call(
        attention,
        (SM, SM) + (VM,) * 7,
        [
            ((width, rows), BF16),
            ((width, rows), BF16),
            ((2 * rows, width), BF16),
            ((2 * rows, width), F32),
            ((2 * rows, width), BF16),
            ((slots, width), BF16),
        ],
        2 * 6 * rows * (3 * rows + half) * width,
        "attention",
        (
            pltpu.VMEM((slots, width), BF16),
            pltpu.VMEM((slots, width), BF16),
            pltpu.VMEM((half, 128), F32),
        ),
    )(tile_clip, dropped, queries, grads, grads_t, kv, from_left, from_right, arrived)
    back = lax.all_to_all(d_slots, "st", split_axis=0, concat_axis=0, tiled=True)
    grad_from_right = lax.ppermute(d_left, "st", down)
    grad_from_left = lax.ppermute(d_right, "st", up)
    out_parts = call(
        out_project,
        (VM, VM),
        [((rows, width), BF16)] * 4,
        2 * rows * width * model,
        "out_project",
    )(attended_t, output_weight)
    groups = lax.axis_size("head")
    swaps = [[(i, i ^ k) for i in range(groups)] for k in range(groups)]
    outs = [out_parts[0]] + [lax.ppermute(out_parts[k], "head", swaps[k]) for k in (1, 2, 3)]
    parts = call(
        input_project,
        (VM,) * 9 + (SM, HBM, HBM),
        [((rows + sound_rows + 16, width), BF16)] * 4,
        2 * (3 * rows + 2 * sound_rows) * width * model,
        "input_project",
        (pltpu.VMEM((3, model, width), BF16), wide, dma),
    )(
        dq_t,
        d_own,
        grad_from_left,
        grad_from_right,
        back,
        video_tokens,
        audio_frames,
        audio_tile,
        modulation,
        tile_clip,
        input_weights,
        audio_weights,
    )
    sums = [parts[0]] + [lax.ppermute(parts[k], "head", swaps[k]) for k in (1, 2, 3)]
    return tuple(
        call(
            finish,
            (VM,) * 4 + (SM,) + (VM,) * 8,
            [((rows, width), BF16), ((rows, width), BF16), ((sound_rows, width), BF16)],
            4 * rows * model,
            "finish",
        )(video_tokens, cotangent, audio_frames, modulation, tile_clip, *outs, *sums)
    )


def solution(mesh):
    return jax.shard_map(
        per_device,
        mesh=mesh,
        in_specs=(
            P("st", None),
            P("st", None),
            P("st", None),
            P(None, None, "head"),
            P(None, None, "head"),
            P("head", None),
            P(),
            P(),
            P(),
            P("st", None),
        ),
        out_specs=(P("st", "head"), P("st", "head"), P("st", "head")),
        check_vma=False,
    )
```

```python
import jax
import jax.numpy as jnp
from jax import lax
from jax.experimental import pallas as pl
from jax.experimental.pallas import tpu as pltpu
from jax.sharding import PartitionSpec as P

HD = 64
EPS = 1e-06
DEAD = -1e30
EMPTY = 32768.0
LOG4 = 1.3862943611198906
F32 = jnp.float32
BF16 = jnp.bfloat16
VMEM_LIMIT = 60 * 1024 * 1024
HEAVY = 10**13

NN = (((1,), (0,)), ((), ()))
NT = (((1,), (1,)), ((), ()))
TN = (((0,), (0,)), ((), ()))


def mm(a, b, dims=NN):
    return lax.dot_general(a, b, dims, preferred_element_type=F32)


def iota(shape, dim):
    return lax.broadcasted_iota(jnp.int32, shape, dim)


def row_scale(matrix):
    return lax.rsqrt(jnp.mean(matrix * matrix, axis=-1, keepdims=True) + EPS)


def to_row(col):
    n = col.shape[0]
    eye = iota((n, n), 0) == iota((n, n), 1)
    return jnp.sum(jnp.where(eye, col, jnp.zeros_like(col)), axis=0, keepdims=True)


def to_col(row):
    n = row.shape[1]
    eye = iota((n, n), 0) == iota((n, n), 1)
    return jnp.sum(jnp.where(eye, row, jnp.zeros_like(row)), axis=1, keepdims=True)


class Source:
    def __init__(self, ref, buf, sems, first, pieces):
        self.buf = buf
        self.copies = []
        self.done = []
        for i, piece in enumerate(pieces):
            src, dst = (ref, buf) if piece is None else (ref.at[piece[0]], buf.at[piece[1]])
            self.copies.append(pltpu.make_async_copy(src, dst, sems.at[first + i]))
            self.done.append(False)

    def start(self):
        for copy in self.copies:
            copy.start()

    def wait(self, i=0):
        if not self.done[i]:
            self.done[i] = True
            self.copies[i].wait()
        return self.buf

    def __getitem__(self, at):
        return self.wait()[at]


class Sink:
    def __init__(self, ref, buf, sem):
        self.buf = buf
        self.shape = buf.shape
        self.dtype = buf.dtype
        self.copy = pltpu.make_async_copy(buf, ref, sem)
        self.started = False

    def __setitem__(self, at, value):
        self.buf[at] = value

    def __getitem__(self, at):
        return self.buf[at]

    def send(self):
        if not self.started:
            self.started = True
            self.copy.start()


class Taken:
    def __init__(self, shape, dtype, pieces=(None,)):
        self.shape, self.dtype, self.pieces = shape, dtype, pieces


SMALL = "small"
RAW = "raw"


def call(body, ins, args, outs, flops, name, scratch=()):
    specs = []
    for spec, arg in zip(ins, args):
        if spec is None:
            spec = Taken(arg.shape, arg.dtype)
        specs.append(spec)
    taken = [spec for spec in specs if isinstance(spec, Taken)]
    n_copies = sum(1 if callable(spec.pieces) else len(spec.pieces) for spec in taken)

    def kernel(*refs):
        refs = list(refs)
        in_refs = refs[: len(specs)]
        out_refs = refs[len(specs) : len(specs) + len(outs)]
        rest = refs[len(specs) + len(outs) :]
        in_bufs = rest[: len(taken)]
        out_bufs = rest[len(taken) : len(taken) + len(outs)]
        in_sems, out_sems = rest[len(taken) + len(outs) : len(taken) + len(outs) + 2]
        extra = rest[len(taken) + len(outs) + 2 :]
        operands, used, first = [], 0, 0
        for spec, ref in zip(specs, in_refs):
            if not isinstance(spec, Taken):
                operands.append(ref)
                continue
            pieces = spec.pieces() if callable(spec.pieces) else spec.pieces
            source = Source(ref, in_bufs[used], in_sems, first, pieces)
            source.start()
            operands.append(source)
            used += 1
            first += len(pieces)
        sinks = [Sink(r, b, out_sems.at[i]) for i, (r, b) in enumerate(zip(out_refs, out_bufs))]
        body(*operands, *sinks, *extra)
        for sink in sinks:
            sink.send()
        for source in operands:
            if isinstance(source, Source):
                for i in range(len(source.copies)):
                    source.wait(i)
        for sink in sinks:
            sink.copy.wait()

    return pl.pallas_call(
        kernel,
        in_specs=[SM if spec == SMALL else HBM for spec in specs],
        out_specs=[HBM] * len(outs),
        out_shape=[jax.ShapeDtypeStruct(shape, dtype) for shape, dtype in outs],
        scratch_shapes=[pltpu.VMEM(spec.shape, spec.dtype) for spec in taken]
        + [pltpu.VMEM(shape, dtype) for shape, dtype in outs]
        + [pltpu.SemaphoreType.DMA((n_copies,)), pltpu.SemaphoreType.DMA((len(outs),))]
        + list(scratch),
        compiler_params=pltpu.CompilerParams(vmem_limit_bytes=VMEM_LIMIT),
        cost_estimate=pl.CostEstimate(flops=flops, bytes_accessed=4 << 20, transcendentals=0),
        name=name,
    )(*args)


SM = pl.BlockSpec(memory_space=pltpu.SMEM)
HBM = pl.BlockSpec(memory_space=pl.ANY)


def my_columns(width):
    return pl.ds(pl.multiple_of(lax.axis_index("head") * width, 128), width)


def modulation_rows(mod, clip_ref):
    clip = clip_ref[lax.axis_index("st")]
    return [mod[i, pl.ds(clip, 1), :] for i in range(3)]


def video_front(tokens, mod, weights, clip_ref, kv, modulated):
    rows = kv.shape[0] // 2
    shifts, scales, _ = modulation_rows(mod, clip_ref)
    inputs = tokens[...].astype(F32)
    hidden = (inputs * row_scale(inputs) * (1.0 + scales) + shifts).astype(BF16)
    modulated[...] = hidden
    modulated.send()
    for i in range(2):
        kv[pl.ds(i * rows, rows), :] = mm(hidden, weights.wait(i)[i]).astype(BF16)


def slot_of(trow, tcol, axis):
    n = trow.shape[1]
    earlier = (tcol == trow) & (iota((n, n), axis) < iota((n, n), 1 - axis))
    rank = jnp.sum(earlier.astype(jnp.int32), axis=axis, keepdims=True)
    return (trow if axis == 0 else tcol) * 8 + rank


def audio_front(audio, targets, weights, after, out):
    sounds = audio[...].astype(F32)
    sound_in = (sounds * row_scale(sounds)).astype(BF16)
    rows = sound_in.shape[0]
    trow = targets[...]
    slot = slot_of(trow, to_col(trow), 0)
    slots = out.shape[0]
    place = iota((slots, rows), 0)
    to_key = (place == slot).astype(BF16)
    to_value = (place == slot + 4).astype(BF16)
    dispatch = jnp.concatenate((to_key, to_value), axis=1)
    filled = jnp.sum(dispatch.astype(F32), axis=1, keepdims=True)
    pairs = [mm(sound_in, weights.wait(i)[i]).astype(BF16) for i in range(2)]
    sent = mm(dispatch, jnp.concatenate(pairs, axis=0))
    shape = sent.shape
    mark = ((iota(shape, 0) & 7) < 4) & (iota(shape, 1) == 0) & (filled < 0.5)
    out[...] = jnp.where(mark, EMPTY, sent).astype(BF16)


def query_front(modulated, cotangent, mod, wq, wo, clip_ref, q, g, gt):
    gating = modulation_rows(mod, clip_ref)[2]
    queries = mm(modulated[...], wq[0]).astype(BF16)
    q[...] = (queries.astype(F32) * (float(HD) ** -0.5)).astype(BF16)
    q.send()
    out_grad = (cotangent[...].astype(F32) * gating).astype(BF16)
    grads = mm(out_grad, wo[...], NT)
    g[...] = grads.astype(BF16)
    g.send()
    gt[...] = grads.T.astype(BF16)


def neighbours(position):
    odd = position & 1
    return position + 1 - 2 * odd, position - 1 + 2 * odd


def attention(q_in, g_in, gt_in, own, near, far, slots_in, clip_ref, dropped_ref,
              at, dq, d_own, d_near, d_far, d_audio, k_all, v_all, bias_ref, sems):
    rows, width = q_in.buf.shape
    slots = slots_in.buf.shape[0]
    half = slots // 2
    loads = []
    for i, ref in enumerate((near, own, far)):
        for j, dst in enumerate((k_all, v_all)):
            src = ref.at[pl.ds(j * rows, rows)]
            loads.append(pltpu.make_async_copy(src, dst.at[pl.ds(i * rows, rows)], sems.at[2 * i + j]))
    for load in loads:
        load.start()
    position = lax.axis_index("st")
    count = clip_ref.shape[0]
    clip = clip_ref[position]

    def side_bias(tile):
        inside = (tile >= 0) & (tile < count)
        other = clip_ref[jnp.clip(tile, 0, count - 1)]
        return jnp.where(inside & (other == clip), -LOG4, DEAD)

    near_bias, far_bias = [side_bias(tile) for tile in neighbours(position)]
    alive = dropped_ref[clip] == 0
    for i, bias in enumerate((near_bias, -LOG4, far_bias)):
        bias_ref[pl.ds(i * rows, rows), :] = jnp.full((rows, 128), bias, F32)
    pick_at = (iota((half, slots), 0) >> 2) * 8 + (iota((half, slots), 0) & 3)
    arrived = slots_in[...]
    for i, dst in enumerate((k_all, v_all)):
        pick = (iota((half, slots), 1) == pick_at + 4 * i).astype(BF16)
        dst[pl.ds(3 * rows, half), :] = mm(pick, arrived).astype(BF16)
    head = k_all[pl.ds(3 * rows, half), pl.ds(0, 128)].astype(F32)
    live = (head[:, 0:1] < EMPTY * 0.5) & alive
    bias_ref[pl.ds(3 * rows, half), :] = jnp.broadcast_to(jnp.where(live, -LOG4, DEAD), (half, 128))
    lane = iota((rows, 128), 1)
    q_ref, g_ref, gt_ref = q_in.wait(), g_in.wait(), gt_in.wait()
    for load in loads:
        load.wait()
    sinks = (d_near, d_own, d_far)
    audio_grads = []
    for pair in range(width // 128):
        cols = slice(pair * 128, (pair + 1) * 128)
        q_pair = q_ref[:, cols]
        g_pair = g_ref[:, cols]
        keys = k_all[:, cols]
        values = v_all[:, cols]
        keys_t = keys.T
        values_t = values.T
        qs, gs, ps, ss = [], [], [], []
        for side in range(2):
            mine = (lane // HD) == side
            half_rows = slice(side * HD, (side + 1) * HD)
            head_rows = slice(pair * 128 + side * HD, pair * 128 + (side + 1) * HD)
            q = jnp.where(mine, q_pair, jnp.zeros_like(q_pair))
            g = jnp.where(mine, g_pair, jnp.zeros_like(g_pair))
            bias = jnp.concatenate([bias_ref[...]] * 2, axis=1)
            weights = jnp.exp(mm(keys, q, NT) + bias)
            inverse = 1.0 / jnp.sum(weights, axis=0, keepdims=True)
            probs = weights * inverse
            rounded = probs.astype(BF16)
            att = mm(values_t[half_rows], rounded).astype(BF16)
            at[head_rows, :] = att
            dots = jnp.sum(att.astype(F32) * gt_ref[head_rows, :].astype(F32), axis=0, keepdims=True)
            score_grad = (probs * (mm(values, g, NT) - dots)).astype(BF16)
            dq[head_rows, :] = (mm(keys_t[half_rows], score_grad) * (float(HD) ** -0.5)).astype(BF16)
            qs.append(q)
            gs.append(g)
            ps.append(rounded)
            ss.append(score_grad)
        d_keys = mm(jnp.concatenate(ss, axis=1), jnp.concatenate(qs, axis=0))
        d_values = mm(jnp.concatenate(ps, axis=1), jnp.concatenate(gs, axis=0))
        for b, sink in enumerate(sinks):
            block = slice(b * rows, (b + 1) * rows)
            sink[pl.ds(0, rows), cols] = d_keys[block].astype(sink.dtype)
            sink[pl.ds(rows, rows), cols] = d_values[block].astype(sink.dtype)
        audio_grads.append((d_keys[3 * rows :].astype(BF16), d_values[3 * rows :].astype(BF16)))
    for i in range(2):
        d_audio[pl.ds(i * half, half), :] = jnp.concatenate([grad[i] for grad in audio_grads], axis=1)


def out_project(d_audio, at, wo, d_slots, to_core, mine, cross):
    rows, width = mine.shape
    slots = d_slots.shape[0]
    half = slots // 2
    back_row = iota((slots, half), 0)
    back_at = (back_row >> 3) * 4 + (back_row & 3)
    total = jnp.zeros((slots, width), F32)
    for i in range(2):
        put = ((iota((slots, half), 1) == back_at) & ((back_row & 4) == 4 * i)).astype(BF16)
        total = total + mm(put, d_audio[pl.ds(i * half, half), :])
    d_slots[...] = total.astype(BF16)
    d_slots.send()
    attended = at[...].astype(F32).T.astype(BF16)
    weights = wo.wait()
    me = lax.axis_index("head")

    def chunk(k):
        cols = pl.ds(pl.multiple_of((me ^ k) * width, 128), width)
        return mm(attended, weights[:, cols]).astype(BF16)

    to_core[pl.ds(0, rows), :] = chunk(1)
    to_core[pl.ds(rows, rows), :] = chunk(3)
    to_core.send()
    mine[...] = chunk(0)
    cross[...] = chunk(2)


def pair_sum_out(mine, cross, arrived, mine_out, cross_out):
    rows = mine_out.shape[0]
    got = arrived.wait()
    cross_out[...] = (cross[...].astype(F32) + got[pl.ds(rows, rows), :].astype(F32)).astype(BF16)
    cross_out.send()
    mine_out[...] = mine[...].astype(F32) + got[pl.ds(0, rows), :].astype(F32)


def finish_out(tokens, mod, mine, cross, clip_ref, out):
    cols = my_columns(out.shape[1])
    gating = mod.wait()[2, pl.ds(clip_ref[lax.axis_index("st")], 1), cols]
    total = mine[...] + cross[...].astype(F32)
    out[...] = (tokens[...].astype(F32) + gating * total).astype(BF16)


def two_terms(row):
    high = row.astype(BF16).astype(F32)
    where_row = iota((16, row.shape[1]), 0)
    return jnp.where(where_row == 0, high, jnp.where(where_row == 1, row - high, 0.0)).astype(BF16)


def input_project(targets, mod, dq, d_own, near, far, back, tokens, audio, weights, audio_weights, clip_ref, after,
                  to_core, mine, cross, scale_out, part_ref):
    rows = tokens.buf.shape[0]
    sound_rows = audio.buf.shape[0]
    both = rows + sound_rows
    width = mine.shape[1]
    me = lax.axis_index("head")
    scales = modulation_rows(mod, clip_ref)[1]
    queries = dq[...].astype(F32).T.astype(BF16)
    pair = (d_own[...] + near[...].astype(F32) + far[...].astype(F32)).astype(BF16)
    trow = targets[...]
    slot = slot_of(trow, to_col(trow), 1)
    arrived = back[...]
    slots = arrived.shape[0]
    sound_grads = []
    for i in range(2):
        pick = (iota((sound_rows, slots), 1) == slot + 4 * i).astype(BF16)
        sound_grads.append(mm(pick, arrived).astype(BF16))
    inputs = tokens[...].astype(F32)
    scale = row_scale(inputs)
    hat = inputs * scale * (1.0 + scales)
    sounds = audio[...].astype(F32)
    sound_scale = row_scale(sounds)
    sound_normed = sounds * sound_scale
    scale_out[pl.ds(0, rows), :] = jnp.broadcast_to(scale, (rows, 128))
    scale_out[pl.ds(rows, sound_rows), :] = jnp.broadcast_to(sound_scale, (sound_rows, 128))
    scale_out.send()
    grads = (queries, pair[:rows], pair[rows:])
    part = sum(mm(grad, weights.wait(i)[i], NT) for i, grad in enumerate(grads)).astype(BF16)
    part_ref[pl.ds(0, rows), :] = part
    dots = jnp.sum(part.astype(F32) * hat, axis=1, keepdims=True)
    part = sum(mm(grad, audio_weights.wait(i)[i], NT) for i, grad in enumerate(sound_grads)).astype(BF16)
    part_ref[pl.ds(rows, sound_rows), :] = part
    sound_dots = jnp.sum(part.astype(F32) * sound_normed, axis=1, keepdims=True)
    extra = two_terms(jnp.concatenate((to_row(dots), to_row(sound_dots)), axis=1))
    for k, sink, first in ((1, to_core, 0), (3, to_core, both + 16), (0, mine, 0), (2, cross, 0)):
        cols = pl.ds(pl.multiple_of((me ^ k) * width, 128), width)
        sink[pl.ds(first, both), :] = part_ref[:, cols]
        sink[pl.ds(first + both, 16), :] = extra
        if k == 3:
            to_core.send()


def pair_sum(mine, cross, arrived, mine_out, cross_out):
    height = mine_out.shape[0]
    both = height - 16
    got = arrived.wait()
    total = cross[...].astype(F32) + got[pl.ds(height, height), :].astype(F32)
    extra = total[both : both + 1] + total[both + 1 : both + 2]
    cross_out[pl.ds(0, both), :] = total[:both].astype(BF16)
    cross_out[pl.ds(both, 16), :] = two_terms(extra)
    cross_out.send()
    mine_out[...] = mine[...].astype(F32) + got[pl.ds(0, height), :].astype(F32)


def finish(tokens, cotangent, audio, scale_in, mod, mine, cross, clip_ref, video_grad, audio_grad):
    rows, width = video_grad.shape
    sound_rows = audio_grad.shape[0]
    both = rows + sound_rows
    model = 4 * width
    cols = my_columns(width)
    scales = mod.wait()[1, pl.ds(clip_ref[lax.axis_index("st")], 1), cols]
    scale = scale_in[...][:, 0:1]
    normed = tokens[...].astype(F32) * scale[:rows]
    sound_normed = audio[...].astype(F32) * scale[rows:]
    total = mine[...] + cross[...].astype(F32)
    row = (total[both : both + 1] + total[both + 1 : both + 2]) * (1.0 / model)
    hat = total[:rows] * (1.0 + scales) - normed * to_col(row[:, :rows])
    video_grad[...] = (cotangent[...].astype(F32) + scale[:rows] * hat).astype(BF16)
    video_grad.send()
    sound_hat = total[rows:both] - sound_normed * to_col(row[:, rows:])
    audio_grad[...] = (scale[rows:] * sound_hat).astype(BF16)


def per_device(
    video_tokens,
    cotangent,
    audio_frames,
    input_weights,
    audio_weights,
    output_weight,
    modulation,
    tile_clip,
    dropped,
    audio_tile,
):
    rows, model = video_tokens.shape
    width = input_weights.shape[2]
    sound_rows = audio_frames.shape[0]
    count = lax.axis_size("st")
    slots = 8 * count
    targets = audio_tile.T
    modulation = jnp.transpose(modulation, (1, 0, 2))

    def layers(first, last):
        pieces = [(pl.ds(i, 1), pl.ds(i - first, 1)) for i in range(first, last)]
        return Taken((last - first, model, width), BF16, pieces)

    def own_block(n):
        return Taken((n, width), BF16, lambda: [((slice(None), my_columns(width)), slice(None))])

    kv, modulated = call(
        video_front,
        (None, None, layers(1, 3), SMALL),
        (video_tokens, modulation, input_weights, tile_clip),
        [((2 * rows, width), BF16), ((rows, model), BF16)],
        2 * rows * model * 2 * width,
        "video_front",
    )
    near_swap = [(i, i ^ 1) for i in range(count)]
    far_swap = [p for i in range(1, count - 2, 2) for p in ((i, i + 1), (i + 1, i))]
    near = lax.ppermute(kv, "st", near_swap)
    far = lax.ppermute(kv, "st", far_swap)
    (sent,) = call(
        audio_front,
        (None, None, layers(0, 2), RAW),
        (audio_frames, targets, audio_weights, kv),
        [((slots, width), BF16)],
        2 * sound_rows * model * 2 * width,
        "audio_front",
    )
    arrived = lax.all_to_all(sent, "st", split_axis=0, concat_axis=0, tiled=True)
    queries, grads, grads_t = call(
        query_front,
        (None, None, None, layers(0, 1), None, SMALL),
        (modulated, cotangent, modulation, input_weights, output_weight, tile_clip),
        [((rows, width), BF16), ((rows, width), BF16), ((width, rows), BF16)],
        HEAVY,
        "query_front",
    )
    half = slots // 2
    attended_t, dq_t, d_own, d_near, d_far, d_audio = call(
        attention,
        (None, None, None, RAW, RAW, RAW, None, SMALL, SMALL),
        (queries, grads, grads_t, kv, near, far, arrived, tile_clip, dropped),
        [
            ((width, rows), BF16),
            ((width, rows), BF16),
            ((2 * rows, width), F32),
            ((2 * rows, width), BF16),
            ((2 * rows, width), BF16),
            ((slots, width), BF16),
        ],
        2 * 6 * rows * (3 * rows + half) * width,
        "attention",
        (
            pltpu.VMEM((3 * rows + half, width), BF16),
            pltpu.VMEM((3 * rows + half, width), BF16),
            pltpu.VMEM((3 * rows + half, 128), F32),
            pltpu.SemaphoreType.DMA((6,)),
        ),
    )
    back_near = lax.ppermute(d_near, "st", near_swap)
    back_far = lax.ppermute(d_far, "st", far_swap)
    groups = lax.axis_size("head")
    core_swap = [(i, i ^ 1) for i in range(groups)]
    cross_swap = [(i, i ^ 2) for i in range(groups)]
    block = ((rows, width), BF16)
    d_slots, to_core, mine, cross = call(
        out_project,
        (None, None, None),
        (d_audio, attended_t, output_weight),
        [((slots, width), BF16), ((2 * rows, width), BF16), block, block],
        HEAVY,
        "out_project",
    )
    back = lax.all_to_all(d_slots, "st", split_axis=0, concat_axis=0, tiled=True)
    out_mine, out_cross = call(
        pair_sum_out,
        (None,) * 3,
        (mine, cross, lax.ppermute(to_core, "head", core_swap)),
        [((rows, width), F32), block],
        HEAVY,
        "pair_sum_out",
    )
    (video_out,) = call(
        finish_out,
        (own_block(rows),) + (None,) * 3 + (SMALL,),
        (video_tokens, modulation, out_mine, lax.ppermute(out_cross, "head", cross_swap), tile_clip),
        [block],
        HEAVY,
        "finish_out",
    )
    height = rows + sound_rows + 16
    block = ((height, width), BF16)
    to_core, mine, cross, scale = call(
        input_project,
        (None,) * 9 + (layers(0, 3), layers(0, 2), SMALL, RAW),
        (
            targets,
            modulation,
            dq_t,
            d_own,
            back_near,
            back_far,
            back,
            video_tokens,
            audio_frames,
            input_weights,
            audio_weights,
            tile_clip,
            out_cross,
        ),
        [((2 * height, width), BF16), block, block, ((rows + sound_rows, 128), F32)],
        2 * (3 * rows + 2 * sound_rows) * width * model,
        "input_project",
        (pltpu.VMEM((rows + sound_rows, model), BF16),),
    )
    mine, cross = call(
        pair_sum,
        (None,) * 3,
        (mine, cross, lax.ppermute(to_core, "head", core_swap)),
        [((height, width), F32), block],
        height * width,
        "pair_sum",
    )
    video_grad, audio_grad = call(
        finish,
        (own_block(rows), own_block(rows), own_block(sound_rows)) + (None,) * 4 + (SMALL,),
        (
            video_tokens,
            cotangent,
            audio_frames,
            scale,
            modulation,
            mine,
            lax.ppermute(cross, "head", cross_swap),
            tile_clip,
        ),
        [((rows, width), BF16), ((sound_rows, width), BF16)],
        4 * rows * model,
        "finish",
    )
    return video_out, video_grad, audio_grad


def solution(mesh):
    return jax.shard_map(
        per_device,
        mesh=mesh,
        in_specs=(
            P("st", None),
            P("st", None),
            P("st", None),
            P(None, None, "head"),
            P(None, None, "head"),
            P("head", None),
            P(),
            P(),
            P(),
            P("st", None),
        ),
        out_specs=(P("st", "head"), P("st", "head"), P("st", "head")),
        check_vma=False,
    )
```

```python
import jax
import jax.numpy as jnp
from jax import lax
from jax.experimental import pallas as pl
from jax.experimental.pallas import tpu as pltpu
from jax.sharding import PartitionSpec as P

HD = 64
EPS = 1e-06
DEAD = -1e30
EMPTY = 32768.0
LOG4 = 1.3862943611198906
F32 = jnp.float32
BF16 = jnp.bfloat16
VMEM_LIMIT = 60 * 1024 * 1024
HEAVY = 10**13

NN = (((1,), (0,)), ((), ()))
NT = (((1,), (1,)), ((), ()))
TN = (((0,), (0,)), ((), ()))


def mm(a, b, dims=NN):
    return lax.dot_general(a, b, dims, preferred_element_type=F32)


def iota(shape, dim):
    return lax.broadcasted_iota(jnp.int32, shape, dim)


def row_scale(matrix):
    return lax.rsqrt(jnp.mean(matrix * matrix, axis=-1, keepdims=True) + EPS)


def to_row(col):
    n = col.shape[0]
    eye = iota((n, n), 0) == iota((n, n), 1)
    return jnp.sum(jnp.where(eye, col, jnp.zeros_like(col)), axis=0, keepdims=True)


def to_col(row):
    n = row.shape[1]
    eye = iota((n, n), 0) == iota((n, n), 1)
    return jnp.sum(jnp.where(eye, row, jnp.zeros_like(row)), axis=1, keepdims=True)


class Source:
    def __init__(self, ref, buf, sems, first, pieces):
        self.buf = buf
        self.copies = []
        self.done = []
        for i, piece in enumerate(pieces):
            src, dst = (ref, buf) if piece is None else (ref.at[piece[0]], buf.at[piece[1]])
            self.copies.append(pltpu.make_async_copy(src, dst, sems.at[first + i]))
            self.done.append(False)

    def start(self, i):
        self.copies[i].start()

    def wait(self, i=0):
        if not self.done[i]:
            self.done[i] = True
            self.copies[i].wait()
        return self.buf

    def __getitem__(self, at):
        return self.wait()[at]


class Sink:
    def __init__(self, ref, buf, sems, first, pieces):
        self.buf = buf
        self.shape = buf.shape
        self.dtype = buf.dtype
        self.copies = []
        self.started = []
        for i, piece in enumerate(pieces):
            src, dst = (buf, ref) if piece is None else (buf.at[piece], ref.at[piece])
            self.copies.append(pltpu.make_async_copy(src, dst, sems.at[first + i]))
            self.started.append(False)

    def __setitem__(self, at, value):
        self.buf[at] = value

    def send(self, i=0):
        if not self.started[i]:
            self.started[i] = True
            self.copies[i].start()


class Taken:
    def __init__(self, shape, dtype, pieces=(None,), space=pltpu.VMEM):
        self.shape, self.dtype, self.pieces, self.space = shape, dtype, pieces, space
        self.count = 1 if callable(pieces) else len(pieces)


RAW = "raw"
HBM = pl.BlockSpec(memory_space=pl.ANY)


def call(body, ins, args, outs, flops, name, scratch=()):
    specs = [Taken(arg.shape, arg.dtype) if spec is None else spec for spec, arg in zip(ins, args)]
    taken = [spec for spec in specs if isinstance(spec, Taken)]
    outs = [out if len(out) == 3 else out + ((None,),) for out in outs]
    n_in = sum(spec.count for spec in taken)
    n_out = sum(len(pieces) for _, _, pieces in outs)

    def kernel(*refs):
        in_refs = refs[: len(specs)]
        out_refs = refs[len(specs) : len(specs) + len(outs)]
        rest = refs[len(specs) + len(outs) :]
        in_bufs = rest[: len(taken)]
        out_bufs = rest[len(taken) : len(taken) + len(outs)]
        in_sems, out_sems = rest[len(taken) + len(outs) : len(taken) + len(outs) + 2]
        extra = rest[len(taken) + len(outs) + 2 :]
        operands, sources, first = [], [], 0
        for spec, ref in zip(specs, in_refs):
            if not isinstance(spec, Taken):
                operands.append(ref)
                continue
            pieces = spec.pieces() if callable(spec.pieces) else spec.pieces
            source = Source(ref, in_bufs[len(sources)], in_sems, first, pieces)
            operands.append(source)
            sources.append(source)
            first += spec.count
        for i in range(max(spec.count for spec in taken)):
            for source in sources:
                if i < len(source.copies):
                    source.start(i)
        sinks, first = [], 0
        for (_, _, pieces), ref, buf in zip(outs, out_refs, out_bufs):
            sinks.append(Sink(ref, buf, out_sems, first, pieces))
            first += len(pieces)
        body(*operands, *sinks, *extra)
        for sink in sinks:
            for i in range(len(sink.copies)):
                sink.send(i)
        for source in sources:
            for i in range(len(source.copies)):
                source.wait(i)
        for sink in sinks:
            for copy in sink.copies:
                copy.wait()

    return pl.pallas_call(
        kernel,
        in_specs=[HBM] * len(specs),
        out_specs=[HBM] * len(outs),
        out_shape=[jax.ShapeDtypeStruct(shape, dtype) for shape, dtype, _ in outs],
        scratch_shapes=[spec.space(spec.shape, spec.dtype) for spec in taken]
        + [pltpu.VMEM(shape, dtype) for shape, dtype, _ in outs]
        + [pltpu.SemaphoreType.DMA((n_in,)), pltpu.SemaphoreType.DMA((n_out,))]
        + list(scratch),
        compiler_params=pltpu.CompilerParams(vmem_limit_bytes=VMEM_LIMIT),
        cost_estimate=pl.CostEstimate(flops=flops, bytes_accessed=4 << 20, transcendentals=0),
        name=name,
    )(*args)


def my_columns(width):
    return pl.ds(pl.multiple_of(lax.axis_index("head") * width, 128), width)


def two_terms(row):
    high = row.astype(BF16).astype(F32)
    where_row = iota((16, row.shape[1]), 0)
    return jnp.where(where_row == 0, high, jnp.where(where_row == 1, row - high, 0.0)).astype(BF16)


def slot_of(trow, tcol, axis):
    n = trow.shape[1]
    earlier = (tcol == trow) & (iota((n, n), axis) < iota((n, n), 1 - axis))
    rank = jnp.sum(earlier.astype(jnp.int32), axis=axis, keepdims=True)
    return (trow if axis == 0 else tcol) * 8 + rank


SHIFTS, SCALES, GATING, NEAR, FAR, SOUND = range(6)


def front(clips, drops, mod, tokens, weights, audio, targets, audio_weights,
          kv, hidden, small, u, scale_out, sound_kv, sent):
    rows = tokens.buf.shape[0]
    sound_rows = audio.buf.shape[0]
    position = lax.axis_index("st")
    count = clips.buf.shape[0]
    clip_ref, dropped_ref = clips.wait(), drops.wait()
    clip = clip_ref[position]
    odd = position & 1

    def side_bias(tile):
        inside = (tile >= 0) & (tile < count)
        other = clip_ref[jnp.clip(tile, 0, count - 1)]
        return jnp.where(inside & (other == clip), -LOG4, DEAD)

    near = side_bias(position + 1 - 2 * odd)
    far = side_bias(position - 1 + 2 * odd)
    sound = jnp.where(dropped_ref[clip] == 0, -LOG4, DEAD)
    shifts, scales, gating = [mod[i, pl.ds(clip, 1), :] for i in range(3)]
    at = iota((8, shifts.shape[1]), 0)
    table = jnp.where(at == SHIFTS, shifts, jnp.where(at == SCALES, scales, gating))
    table = jnp.where(at == NEAR, near, jnp.where(at == FAR, far, table))
    small[...] = jnp.where(at == SOUND, sound, table)
    small.send()
    inputs = tokens[...].astype(F32)
    scale = row_scale(inputs)
    both = jnp.concatenate(
        ((inputs * scale * (1.0 + scales) + shifts).astype(BF16), two_terms(shifts)), axis=0
    )
    for i in range(2):
        block = pl.ds(i * rows, rows)
        made = mm(both, weights.wait(i)[i])
        kv[block, :] = made[:rows].astype(BF16)
        u[block, :] = (made[:rows] - (made[rows : rows + 1] + made[rows + 1 : rows + 2])).astype(BF16)
    kv.send()
    u.send()
    hidden[...] = both
    hidden.send()
    sounds = audio[...].astype(F32)
    sound_scale = row_scale(sounds)
    scale_out[pl.ds(0, rows), :] = jnp.broadcast_to(scale, (rows, 128))
    scale_out[pl.ds(rows, sound_rows), :] = jnp.broadcast_to(sound_scale, (sound_rows, 128))
    scale_out.send()
    sound_in = (sounds * sound_scale).astype(BF16)
    trow = targets[...]
    slot = slot_of(trow, to_col(trow), 0)
    slots = sent.shape[0]
    place = iota((slots, sound_rows), 0)
    dispatch = jnp.concatenate((place == slot, place == slot + 4), axis=1).astype(BF16)
    filled = jnp.sum(dispatch.astype(F32), axis=1, keepdims=True)
    pairs = [mm(sound_in, audio_weights.wait(i)[i]).astype(BF16) for i in range(2)]
    pairs = jnp.concatenate(pairs, axis=0)
    sound_kv[...] = pairs
    sound_kv.send()
    made = mm(dispatch, pairs)
    mark = ((iota(made.shape, 0) & 7) < 4) & (iota(made.shape, 1) == 0) & (filled < 0.5)
    sent[...] = jnp.where(mark, EMPTY, made).astype(BF16)


def query_front(hidden, wq, cotangent, small, wo, q, uq, g, gt):
    rows = q.shape[0]
    made = mm(hidden[...], wq[0])
    queries = made[:rows].astype(BF16)
    q[...] = (queries.astype(F32) * (float(HD) ** -0.5)).astype(BF16)
    q.send()
    uq[...] = (made[:rows] - (made[rows : rows + 1] + made[rows + 1 : rows + 2])).astype(BF16)
    uq.send()
    out_grad = (cotangent[...].astype(F32) * small[GATING : GATING + 1, :]).astype(BF16)
    grads = mm(out_grad, wo[...], NT)
    g[...] = grads.astype(BF16)
    g.send()
    gt[...] = grads.T.astype(BF16)


def attention(small, slots_in, q_in, g_in, gt_in, near, own, far,
              at, dq, d_own, d_near, d_far, d_audio, k_all, v_all, bias_ref):
    rows, width = q_in.buf.shape
    slots = slots_in.buf.shape[0]
    half = slots // 2
    table = small[:, 0:128]
    for i, bias in enumerate((table[NEAR : NEAR + 1], None, table[FAR : FAR + 1])):
        bias = jnp.full((1, 128), -LOG4, F32) if bias is None else bias
        bias_ref[pl.ds(i * rows, rows), :] = jnp.broadcast_to(bias, (rows, 128))
    pick_at = (iota((half, slots), 0) >> 2) * 8 + (iota((half, slots), 0) & 3)
    picks = [(iota((half, slots), 1) == pick_at + 4 * i).astype(BF16) for i in range(2)]
    lane = iota((rows, 128), 1)
    sinks = (d_near, d_own, d_far)
    tail = pl.ds(3 * rows, half)
    for pair in range(width // 128):
        cols = slice(pair * 128, (pair + 1) * 128)
        arrived = slots_in.wait(pair)[:, cols]
        k_all[tail, cols] = mm(picks[0], arrived).astype(BF16)
        v_all[tail, cols] = mm(picks[1], arrived).astype(BF16)
        if pair == 0:
            live = k_all[tail, cols].astype(F32)[:, 0:1] < EMPTY * 0.5
            sound = jnp.broadcast_to(table[SOUND : SOUND + 1], (half, 128))
            bias_ref[tail, :] = jnp.where(live, sound, DEAD)
        q_pair = q_in.wait(pair)[:, cols]
        g_pair = g_in.wait(pair)[:, cols]
        gt_pair = gt_in.wait(pair)[cols, :]
        for i, source in enumerate((near, own, far)):
            block = pl.ds(i * rows, rows)
            got = source.wait(pair)
            k_all[block, cols] = got[pl.ds(0, rows), cols]
            v_all[block, cols] = got[pl.ds(rows, rows), cols]
        keys = k_all[:, cols]
        values = v_all[:, cols]
        keys_t = keys.T
        values_t = values.T
        qs, gs, ps, ss = [], [], [], []
        for side in range(2):
            mine = (lane // HD) == side
            half_rows = slice(side * HD, (side + 1) * HD)
            head_rows = slice(pair * 128 + side * HD, pair * 128 + (side + 1) * HD)
            q = jnp.where(mine, q_pair, jnp.zeros_like(q_pair))
            g = jnp.where(mine, g_pair, jnp.zeros_like(g_pair))
            bias = jnp.concatenate([bias_ref[...]] * 2, axis=1)
            weights = jnp.exp(mm(keys, q, NT) + bias)
            inverse = 1.0 / jnp.sum(weights, axis=0, keepdims=True)
            probs = weights * inverse
            rounded = probs.astype(BF16)
            att = mm(values_t[half_rows], rounded).astype(BF16)
            at[head_rows, :] = att
            dots = jnp.sum(att.astype(F32) * gt_pair[half_rows].astype(F32), axis=0, keepdims=True)
            score_grad = (probs * (mm(values, g, NT) - dots)).astype(BF16)
            dq[head_rows, :] = (mm(keys_t[half_rows], score_grad) * (float(HD) ** -0.5)).astype(BF16)
            qs.append(q)
            gs.append(g)
            ps.append(rounded)
            ss.append(score_grad)
        d_keys = mm(jnp.concatenate(ss, axis=1), jnp.concatenate(qs, axis=0))
        d_values = mm(jnp.concatenate(ps, axis=1), jnp.concatenate(gs, axis=0))
        for b, sink in enumerate(sinks):
            block = slice(b * rows, (b + 1) * rows)
            sink[pl.ds(0, rows), cols] = d_keys[block].astype(sink.dtype)
            sink[pl.ds(rows, rows), cols] = d_values[block].astype(sink.dtype)
        d_audio[pl.ds(0, half), cols] = d_keys[3 * rows :].astype(BF16)
        d_audio[pl.ds(half, half), cols] = d_values[3 * rows :].astype(BF16)
        for sink in (at, dq, d_own, d_near, d_far, d_audio):
            sink.send(pair)


def group_block(weights, k, width):
    return weights[:, pl.ds(pl.multiple_of((lax.axis_index("head") ^ k) * width, 128), width)]


def out_first(d_audio, at, wo, d_slots, to_core, keep):
    slots, width = d_slots.shape
    half = slots // 2
    rows = at.buf.shape[1]
    back_row = iota((slots, half), 0)
    back_at = (back_row >> 3) * 4 + (back_row & 3)
    total = jnp.zeros((slots, width), F32)
    for i in range(2):
        put = ((iota((slots, half), 1) == back_at) & ((back_row & 4) == 4 * i)).astype(BF16)
        total = total + mm(put, d_audio[pl.ds(i * half, half), :])
    d_slots[...] = total.astype(BF16)
    d_slots.send()
    attended = at[...].astype(F32).T.astype(BF16)
    for sink, blocks in ((to_core, (1, 3)), (keep, (0, 2))):
        for i, k in enumerate(blocks):
            part = mm(attended, group_block(wo.wait(), k, width))
            sink[pl.ds(i * rows, rows), :] = part.astype(BF16)
        sink.send()


def head_blocks(part_ref, extra, to_core, keep):
    rows = part_ref.shape[0]
    width = to_core.shape[1]
    me = lax.axis_index("head")
    for sink, blocks in ((to_core, (1, 3)), (keep, (0, 2))):
        for i, k in enumerate(blocks):
            cols = pl.ds(pl.multiple_of((me ^ k) * width, 128), width)
            sink[pl.ds(i * (rows + 16), rows), :] = part_ref[:, cols]
            sink[pl.ds(i * (rows + 16) + rows, 16), :] = extra
        sink.send()


def extra_rows(dots, width):
    row = to_row(jnp.sum(dots, axis=1, keepdims=True))
    row = jnp.concatenate((row, jnp.zeros((1, width - row.shape[1]), F32)), axis=1)
    return two_terms(row)


def video_project(dq, d_own, near, far, uq, u, weights, after, to_core, keep, part_ref):
    rows, width = uq.buf.shape
    queries = dq[...].astype(F32).T.astype(BF16)
    pair = (d_own[...].astype(F32) + near[...].astype(F32) + far[...].astype(F32)).astype(BF16)
    grads = (queries, pair[:rows], pair[rows:])
    others = (uq[...], u[pl.ds(0, rows), :], u[pl.ds(rows, rows), :])
    dots = sum(grad.astype(F32) * other.astype(F32) for grad, other in zip(grads, others))
    extra = extra_rows(dots, width)
    part = sum(mm(grad, weights.wait(i)[i], NT) for i, grad in enumerate(grads))
    part_ref[...] = part.astype(BF16)
    head_blocks(part_ref, extra, to_core, keep)


def sound_project(targets, back, sound_kv, audio_weights, to_core, keep, part_ref):
    rows = targets.buf.shape[1]
    width = to_core.shape[1]
    trow = targets[...]
    slot = slot_of(trow, to_col(trow), 1)
    arrived = back[...]
    slots = arrived.shape[0]
    grads = []
    for i in range(2):
        pick = (iota((rows, slots), 1) == slot + 4 * i).astype(BF16)
        grads.append(mm(pick, arrived).astype(BF16))
    others = (sound_kv[pl.ds(0, rows), :], sound_kv[pl.ds(rows, rows), :])
    dots = sum(grad.astype(F32) * other.astype(F32) for grad, other in zip(grads, others))
    extra = extra_rows(dots, width)
    part = sum(mm(grad, audio_weights.wait(i)[i], NT) for i, grad in enumerate(grads))
    part_ref[...] = part.astype(BF16)
    head_blocks(part_ref, extra, to_core, keep)


def pair_sum(*refs):
    cross, mine = refs[-2:]
    first = 0
    for keep, arrived in zip(refs[:-2:2], refs[1:-2:2]):
        tall = keep.buf.shape[0] // 2
        own, other = pl.ds(0, tall), pl.ds(tall, tall)
        block = pl.ds(first, tall)
        total = keep[other, :].astype(F32) + arrived[other, :].astype(F32)
        cross[block, :] = total.astype(BF16)
        if first + tall == mine.shape[0]:
            extra = total[tall - 16 : tall - 15] + total[tall - 15 : tall - 14]
            cross[pl.ds(first + tall - 16, 16), :] = two_terms(extra)
            cross.send()
        mine[block, :] = keep[own, :].astype(F32) + arrived[own, :].astype(F32)
        first += tall


def finish(tokens, audio, cotangent, scale_in, small, mine, cross, sound_mine, sound_cross,
           video_out, video_grad, audio_grad):
    rows, width = video_grad.shape
    sound_rows = audio_grad.shape[0]
    scale = scale_in[...][:, 0:1]

    def mean_of(total, count):
        row = (total[count : count + 1] + total[count + 1 : count + 2])[:, :count]
        return to_col(row * (1.0 / (4 * width)))

    inputs = tokens[...].astype(F32)
    normed = inputs * scale[:rows]
    video = mine[...] + cross[...].astype(F32)
    video_out[...] = (inputs + small[GATING : GATING + 1, :] * video[:rows]).astype(BF16)
    video_out.send()
    video = video[rows:]
    hat = video[:rows] * (1.0 + small[SCALES : SCALES + 1, :]) - normed * mean_of(video, rows)
    video_grad[...] = (cotangent[...].astype(F32) + scale[:rows] * hat).astype(BF16)
    video_grad.send()
    normed = audio[...].astype(F32) * scale[rows:]
    sound = sound_mine[...] + sound_cross[...].astype(F32)
    hat = sound[:sound_rows] - normed * mean_of(sound, sound_rows)
    audio_grad[...] = (scale[rows:] * hat).astype(BF16)


def per_device(
    video_tokens,
    cotangent,
    audio_frames,
    input_weights,
    audio_weights,
    output_weight,
    modulation,
    tile_clip,
    dropped,
    audio_tile,
):
    rows, model = video_tokens.shape
    width = input_weights.shape[2]
    sound_rows = audio_frames.shape[0]
    count = lax.axis_size("st")
    slots = 8 * count
    half = slots // 2
    pairs = width // 128
    targets = audio_tile.T
    modulation = jnp.transpose(modulation, (1, 0, 2))
    columns = [(slice(None), pl.ds(p * 128, 128)) for p in range(pairs)]
    head_rows = [(pl.ds(p * 128, 128), slice(None)) for p in range(pairs)]

    def layers(first, last):
        pieces = [(pl.ds(i, 1), pl.ds(i - first, 1)) for i in range(first, last)]
        return Taken((last - first, model, width), BF16, pieces)

    def own_block(n, dtype=BF16):
        return Taken((n, width), dtype, lambda: [((slice(None), my_columns(width)), slice(None))])

    def scalars(arg):
        return Taken(arg.shape, arg.dtype, space=pltpu.SMEM)

    def split(arg, pieces):
        return Taken(arg.shape, arg.dtype, [(piece, piece) for piece in pieces])

    kv, hidden, small, u, scale, sound_kv, sent = call(
        front,
        (scalars(tile_clip), scalars(dropped), None, None, layers(1, 3), None, None, layers(0, 2)),
        (tile_clip, dropped, modulation, video_tokens, input_weights, audio_frames, targets, audio_weights),
        [
            ((2 * rows, width), BF16),
            ((rows + 16, model), BF16),
            ((8, model), F32),
            ((2 * rows, width), BF16),
            ((rows + sound_rows, 128), F32),
            ((2 * sound_rows, width), BF16),
            ((slots, width), BF16),
        ],
        2 * (rows + sound_rows) * model * 2 * width,
        "front",
    )
    near_swap = [(i, i ^ 1) for i in range(count)]
    far_swap = [p for i in range(1, count - 2, 2) for p in ((i, i + 1), (i + 1, i))]
    near = lax.ppermute(kv, "st", near_swap)
    far = lax.ppermute(kv, "st", far_swap)
    arrived = lax.all_to_all(sent, "st", split_axis=0, concat_axis=0, tiled=True)
    block = ((rows, width), BF16)
    queries, uq, grads, grads_t = call(
        query_front,
        (None, layers(0, 1), None, None, None),
        (hidden, input_weights, cotangent, small, output_weight),
        [block, block, block, ((width, rows), BF16)],
        HEAVY,
        "query_front",
    )
    attended_t, dq_t, d_own, d_near, d_far, d_audio = call(
        attention,
        (None, split(arrived, columns), split(queries, columns), split(grads, columns))
        + (split(grads_t, head_rows),)
        + (split(kv, columns),) * 3,
        (small, arrived, queries, grads, grads_t, near, kv, far),
        [
            ((width, rows), BF16, head_rows),
            ((width, rows), BF16, head_rows),
            ((2 * rows, width), BF16, columns),
            ((2 * rows, width), BF16, columns),
            ((2 * rows, width), BF16, columns),
            ((slots, width), BF16, columns),
        ],
        2 * 6 * rows * (3 * rows + half) * width,
        "attention",
        (
            pltpu.VMEM((3 * rows + half, width), BF16),
            pltpu.VMEM((3 * rows + half, width), BF16),
            pltpu.VMEM((3 * rows + half, 128), F32),
        ),
    )
    back_near = lax.ppermute(d_near, "st", near_swap)
    back_far = lax.ppermute(d_far, "st", far_swap)
    groups = lax.axis_size("head")
    core_swap = [(i, i ^ 1) for i in range(groups)]
    cross_swap = [(i, i ^ 2) for i in range(groups)]
    two = ((2 * rows, width), BF16)
    d_slots, out_to_core, out_keep = call(
        out_first,
        (None, None, None),
        (d_audio, attended_t, output_weight),
        [((slots, width), BF16), two, two],
        HEAVY,
        "out_first",
    )
    back = lax.all_to_all(d_slots, "st", split_axis=0, concat_axis=0, tiled=True)
    out_from_core = lax.ppermute(out_to_core, "head", core_swap)

    def head_sum(body, ins, args, n, cost, name, before=(), above=0):
        both = ((2 * (n + 16), width), BF16)
        scratch = (pltpu.VMEM((n, model), BF16),)
        to_core, keep = call(body, ins, args, [both, both], cost, name, scratch)
        cross, mine = call(
            pair_sum,
            (None,) * (2 + len(before)),
            (*before, keep, lax.ppermute(to_core, "head", core_swap)),
            [((above + n + 16, width), BF16), ((above + n + 16, width), F32)],
            rows * width,
            name + "_sum",
        )
        return mine, lax.ppermute(cross, "head", cross_swap)

    video = head_sum(
        video_project,
        (None,) * 6 + (layers(0, 3), RAW),
        (dq_t, d_own, back_near, back_far, uq, u, input_weights, out_from_core),
        rows,
        HEAVY,
        "video",
        (out_keep, out_from_core),
        rows,
    )
    sound = head_sum(
        sound_project,
        (None,) * 3 + (layers(0, 2),),
        (targets, back, sound_kv, audio_weights),
        sound_rows,
        10**9,
        "sound",
    )
    return call(
        finish,
        (own_block(rows), own_block(sound_rows), own_block(rows), None, own_block(8, F32)) + (None,) * 4,
        (video_tokens, audio_frames, cotangent, scale, small, *video, *sound),
        [((rows, width), BF16), ((rows, width), BF16), ((sound_rows, width), BF16)],
        4 * rows * width,
        "finish",
    )


def solution(mesh):
    return jax.shard_map(
        per_device,
        mesh=mesh,
        in_specs=(
            P("st", None),
            P("st", None),
            P("st", None),
            P(None, None, "head"),
            P(None, None, "head"),
            P("head", None),
            P(),
            P(),
            P(),
            P("st", None),
        ),
        out_specs=(P("st", "head"), P("st", "head"), P("st", "head")),
        check_vma=False,
    )
```

```python
import jax
import jax.numpy as jnp
from jax import lax
from jax.experimental import pallas as pl
from jax.experimental.pallas import tpu as pltpu
from jax.sharding import PartitionSpec as P

HD = 64
EPS = 1e-06
DEAD = -1e30
EMPTY = 32768.0
LOG4 = 1.3862943611198906
F32 = jnp.float32
BF16 = jnp.bfloat16
VMEM_LIMIT = 60 * 1024 * 1024
HEAVY = 10**13

NN = (((1,), (0,)), ((), ()))
NT = (((1,), (1,)), ((), ()))
TN = (((0,), (0,)), ((), ()))


def mm(a, b, dims=NN):
    return lax.dot_general(a, b, dims, preferred_element_type=F32)


def iota(shape, dim):
    return lax.broadcasted_iota(jnp.int32, shape, dim)


def row_scale(matrix):
    return lax.rsqrt(jnp.mean(matrix * matrix, axis=-1, keepdims=True) + EPS)


def to_row(col):
    n = col.shape[0]
    eye = iota((n, n), 0) == iota((n, n), 1)
    return jnp.sum(jnp.where(eye, col, jnp.zeros_like(col)), axis=0, keepdims=True)


def to_col(row):
    n = row.shape[1]
    eye = iota((n, n), 0) == iota((n, n), 1)
    return jnp.sum(jnp.where(eye, row, jnp.zeros_like(row)), axis=1, keepdims=True)


class Source:
    def __init__(self, ref, buf, sems, first, pieces):
        self.buf = buf
        self.copies = []
        self.done = []
        for i, piece in enumerate(pieces):
            src, dst = (ref, buf) if piece is None else (ref.at[piece[0]], buf.at[piece[1]])
            self.copies.append(pltpu.make_async_copy(src, dst, sems.at[first + i]))
            self.done.append(False)

    def start(self, i):
        self.copies[i].start()

    def wait(self, i=0):
        if not self.done[i]:
            self.done[i] = True
            self.copies[i].wait()
        return self.buf

    def __getitem__(self, at):
        return self.wait()[at]


class Sink:
    def __init__(self, ref, buf, sems, first, pieces):
        self.buf = buf
        self.shape = buf.shape
        self.dtype = buf.dtype
        self.copies = []
        self.started = []
        for i, piece in enumerate(pieces):
            src, dst = (buf, ref) if piece is None else (buf.at[piece], ref.at[piece])
            self.copies.append(pltpu.make_async_copy(src, dst, sems.at[first + i]))
            self.started.append(False)

    def __setitem__(self, at, value):
        self.buf[at] = value

    def send(self, i=0):
        if not self.started[i]:
            self.started[i] = True
            self.copies[i].start()


class Taken:
    def __init__(self, shape, dtype, pieces=(None,), space=pltpu.VMEM):
        self.shape, self.dtype, self.pieces, self.space = shape, dtype, pieces, space
        self.count = 1 if callable(pieces) else len(pieces)


RAW = "raw"
HBM = pl.BlockSpec(memory_space=pl.ANY)


def call(body, ins, args, outs, flops, name, scratch=()):
    specs = [Taken(arg.shape, arg.dtype) if spec is None else spec for spec, arg in zip(ins, args)]
    taken = [spec for spec in specs if isinstance(spec, Taken)]
    outs = [out if len(out) == 3 else out + ((None,),) for out in outs]
    n_in = sum(spec.count for spec in taken)
    n_out = sum(len(pieces) for _, _, pieces in outs)

    def kernel(*refs):
        in_refs = refs[: len(specs)]
        out_refs = refs[len(specs) : len(specs) + len(outs)]
        rest = refs[len(specs) + len(outs) :]
        in_bufs = rest[: len(taken)]
        out_bufs = rest[len(taken) : len(taken) + len(outs)]
        in_sems, out_sems = rest[len(taken) + len(outs) : len(taken) + len(outs) + 2]
        extra = rest[len(taken) + len(outs) + 2 :]
        operands, sources, first = [], [], 0
        for spec, ref in zip(specs, in_refs):
            if not isinstance(spec, Taken):
                operands.append(ref)
                continue
            pieces = spec.pieces() if callable(spec.pieces) else spec.pieces
            source = Source(ref, in_bufs[len(sources)], in_sems, first, pieces)
            operands.append(source)
            sources.append(source)
            first += spec.count
        for i in range(max(spec.count for spec in taken)):
            for source in sources:
                if i < len(source.copies):
                    source.start(i)
        sinks, first = [], 0
        for (_, _, pieces), ref, buf in zip(outs, out_refs, out_bufs):
            sinks.append(Sink(ref, buf, out_sems, first, pieces))
            first += len(pieces)
        body(*operands, *sinks, *extra)
        for sink in sinks:
            for i in range(len(sink.copies)):
                sink.send(i)
        for source in sources:
            for i in range(len(source.copies)):
                source.wait(i)
        for sink in sinks:
            for copy in sink.copies:
                copy.wait()

    return pl.pallas_call(
        kernel,
        in_specs=[HBM] * len(specs),
        out_specs=[HBM] * len(outs),
        out_shape=[jax.ShapeDtypeStruct(shape, dtype) for shape, dtype, _ in outs],
        scratch_shapes=[spec.space(spec.shape, spec.dtype) for spec in taken]
        + [pltpu.VMEM(shape, dtype) for shape, dtype, _ in outs]
        + [pltpu.SemaphoreType.DMA((n_in,)), pltpu.SemaphoreType.DMA((n_out,))]
        + list(scratch),
        compiler_params=pltpu.CompilerParams(vmem_limit_bytes=VMEM_LIMIT),
        cost_estimate=pl.CostEstimate(flops=flops, bytes_accessed=4 << 20, transcendentals=0),
        name=name,
    )(*args)


def my_columns(width):
    return pl.ds(pl.multiple_of(lax.axis_index("head") * width, 128), width)


def two_terms(row):
    high = row.astype(BF16).astype(F32)
    where_row = iota((16, row.shape[1]), 0)
    return jnp.where(where_row == 0, high, jnp.where(where_row == 1, row - high, 0.0)).astype(BF16)


def slot_of(trow, tcol, axis):
    n = trow.shape[1]
    earlier = (tcol == trow) & (iota((n, n), axis) < iota((n, n), 1 - axis))
    rank = jnp.sum(earlier.astype(jnp.int32), axis=axis, keepdims=True)
    return (trow if axis == 0 else tcol) * 8 + rank


SHIFTS, SCALES, GATING, NEAR, FAR, SOUND = range(6)


def front(clips, drops, mod, tokens, weights, audio, targets, audio_weights,
          kv, hidden, small, u, scale_out, sound_kv, sent):
    rows = tokens.buf.shape[0]
    sound_rows = audio.buf.shape[0]
    position = lax.axis_index("st")
    count = clips.buf.shape[0]
    clip_ref, dropped_ref = clips.wait(), drops.wait()
    clip = clip_ref[position]
    odd = position & 1

    def side_bias(tile):
        inside = (tile >= 0) & (tile < count)
        other = clip_ref[jnp.clip(tile, 0, count - 1)]
        return jnp.where(inside & (other == clip), -LOG4, DEAD)

    near = side_bias(position + 1 - 2 * odd)
    far = side_bias(position - 1 + 2 * odd)
    sound = jnp.where(dropped_ref[clip] == 0, -LOG4, DEAD)
    shifts, scales, gating = [mod[i, pl.ds(clip, 1), :] for i in range(3)]
    at = iota((8, shifts.shape[1]), 0)
    table = jnp.where(at == SHIFTS, shifts, jnp.where(at == SCALES, scales, gating))
    table = jnp.where(at == NEAR, near, jnp.where(at == FAR, far, table))
    small[...] = jnp.where(at == SOUND, sound, table)
    small.send()
    inputs = tokens[...].astype(F32)
    scale = row_scale(inputs)
    both = jnp.concatenate(
        ((inputs * scale * (1.0 + scales) + shifts).astype(BF16), two_terms(shifts)), axis=0
    )
    for i in range(2):
        block = pl.ds(i * rows, rows)
        made = mm(both, weights.wait(i)[i])
        kv[block, :] = made[:rows].astype(BF16)
        u[block, :] = (made[:rows] - (made[rows : rows + 1] + made[rows + 1 : rows + 2])).astype(BF16)
    kv.send()
    u.send()
    hidden[...] = both
    hidden.send()
    sounds = audio[...].astype(F32)
    sound_scale = row_scale(sounds)
    scale_out[pl.ds(0, rows), :] = jnp.broadcast_to(scale, (rows, 128))
    scale_out[pl.ds(rows, sound_rows), :] = jnp.broadcast_to(sound_scale, (sound_rows, 128))
    scale_out.send()
    sound_in = (sounds * sound_scale).astype(BF16)
    trow = targets[...]
    slot = slot_of(trow, to_col(trow), 0)
    slots = sent.shape[0]
    place = iota((slots, sound_rows), 0)
    dispatch = jnp.concatenate((place == slot, place == slot + 4), axis=1).astype(BF16)
    filled = jnp.sum(dispatch.astype(F32), axis=1, keepdims=True)
    pairs = [mm(sound_in, audio_weights.wait(i)[i]).astype(BF16) for i in range(2)]
    pairs = jnp.concatenate(pairs, axis=0)
    sound_kv[...] = pairs
    sound_kv.send()
    made = mm(dispatch, pairs)
    mark = ((iota(made.shape, 0) & 7) < 4) & (iota(made.shape, 1) == 0) & (filled < 0.5)
    sent[...] = jnp.where(mark, EMPTY, made).astype(BF16)


def query_front(hidden, wq, cotangent, small, wo, q, uq, g, gt):
    rows = q.shape[0]
    made = mm(hidden[...], wq[0])
    queries = made[:rows].astype(BF16)
    q[...] = (queries.astype(F32) * (float(HD) ** -0.5)).astype(BF16)
    q.send()
    uq[...] = (made[:rows] - (made[rows : rows + 1] + made[rows + 1 : rows + 2])).astype(BF16)
    uq.send()
    out_grad = (cotangent[...].astype(F32) * small[GATING : GATING + 1, :]).astype(BF16)
    grads = mm(out_grad, wo[...], NT)
    g[...] = grads.astype(BF16)
    g.send()
    gt[...] = grads.T.astype(BF16)


def attention(small, slots_in, q_in, g_in, gt_in, near, own, far,
              at, dq, d_own, d_near, d_far, d_audio, k_all, v_all, bias_ref):
    rows, width = q_in.buf.shape
    slots = slots_in.buf.shape[0]
    half = slots // 2
    table = small[:, 0:128]
    for i, bias in enumerate((table[NEAR : NEAR + 1], None, table[FAR : FAR + 1])):
        bias = jnp.full((1, 128), -LOG4, F32) if bias is None else bias
        bias_ref[pl.ds(i * rows, rows), :] = jnp.broadcast_to(bias, (rows, 128))
    pick_at = (iota((half, slots), 0) >> 2) * 8 + (iota((half, slots), 0) & 3)
    picks = [(iota((half, slots), 1) == pick_at + 4 * i).astype(BF16) for i in range(2)]
    lane = iota((rows, 128), 1)
    sinks = (d_near, d_own, d_far)
    tail = pl.ds(3 * rows, half)
    saved = []
    for pair in range(width // 128):
        cols = slice(pair * 128, (pair + 1) * 128)
        arrived = slots_in.wait(pair)[:, cols]
        k_all[tail, cols] = mm(picks[0], arrived).astype(BF16)
        v_all[tail, cols] = mm(picks[1], arrived).astype(BF16)
        if pair == 0:
            live = k_all[tail, cols].astype(F32)[:, 0:1] < EMPTY * 0.5
            sound = jnp.broadcast_to(table[SOUND : SOUND + 1], (half, 128))
            bias_ref[tail, :] = jnp.where(live, sound, DEAD)
        q_pair = q_in.wait(pair)[:, cols]
        g_pair = g_in.wait(pair)[:, cols]
        gt_pair = gt_in.wait(pair)[cols, :]
        for i, source in enumerate((near, own, far)):
            block = pl.ds(i * rows, rows)
            got = source.wait(pair)
            k_all[block, cols] = got[pl.ds(0, rows), cols]
            v_all[block, cols] = got[pl.ds(rows, rows), cols]
        keys = k_all[:, cols]
        values = v_all[:, cols]
        keys_t = keys.T
        values_t = values.T
        qs, gs, ps, ss = [], [], [], []
        bias = jnp.concatenate([bias_ref[...]] * 2, axis=1)
        for side in range(2):
            mine = (lane // HD) == side
            qs.append(jnp.where(mine, q_pair, jnp.zeros_like(q_pair)))
            gs.append(jnp.where(mine, g_pair, jnp.zeros_like(g_pair)))
        scores = mm(keys, jnp.concatenate(qs, axis=0), NT)
        scores = [scores[:, :rows], scores[:, rows:]]
        grads = mm(values, jnp.concatenate(gs, axis=0), NT)
        grads = [grads[:, :rows], grads[:, rows:]]
        probs = []
        for side in range(2):
            weights = jnp.exp(scores[side] + bias)
            probs.append(weights * (1.0 / jnp.sum(weights, axis=0, keepdims=True)))
            ps.append(probs[side].astype(BF16))
        atts = [mm(values_t[i * HD : (i + 1) * HD], ps[i]).astype(BF16) for i in range(2)]
        saved.append((cols, keys, values, keys_t, qs, gs, ps, ss, probs, grads, atts, gt_pair))
    for pair, (cols, keys, values, keys_t, qs, gs, ps, ss, probs, grads, atts, gt_pair) in enumerate(saved):
        for side in range(2):
            half_rows = slice(side * HD, (side + 1) * HD)
            head_rows = slice(pair * 128 + side * HD, pair * 128 + (side + 1) * HD)
            at[head_rows, :] = atts[side]
            dots = jnp.sum(atts[side].astype(F32) * gt_pair[half_rows].astype(F32), axis=0, keepdims=True)
            ss.append((probs[side] * (grads[side] - dots)).astype(BF16))
        for side in range(2):
            half_rows = slice(side * HD, (side + 1) * HD)
            head_rows = slice(pair * 128 + side * HD, pair * 128 + (side + 1) * HD)
            dqs = mm(keys_t[half_rows], ss[side]) * (float(HD) ** -0.5)
            dq[head_rows, :] = dqs.astype(BF16)
        d_keys = mm(jnp.concatenate(ss, axis=1), jnp.concatenate(qs, axis=0))
        d_values = mm(jnp.concatenate(ps, axis=1), jnp.concatenate(gs, axis=0))
        for b, sink in enumerate(sinks):
            block = slice(b * rows, (b + 1) * rows)
            sink[pl.ds(0, rows), cols] = d_keys[block].astype(sink.dtype)
            sink[pl.ds(rows, rows), cols] = d_values[block].astype(sink.dtype)
        d_audio[pl.ds(0, half), cols] = d_keys[3 * rows :].astype(BF16)
        d_audio[pl.ds(half, half), cols] = d_values[3 * rows :].astype(BF16)
        for sink in (at, dq, d_own, d_near, d_far, d_audio):
            sink.send(pair)


def group_block(weights, k, width):
    return weights[:, pl.ds(pl.multiple_of((lax.axis_index("head") ^ k) * width, 128), width)]


def out_first(d_audio, at, wo, d_slots, to_core, keep):
    slots, width = d_slots.shape
    half = slots // 2
    rows = at.buf.shape[1]
    back_row = iota((slots, half), 0)
    back_at = (back_row >> 3) * 4 + (back_row & 3)
    total = jnp.zeros((slots, width), F32)
    for i in range(2):
        put = ((iota((slots, half), 1) == back_at) & ((back_row & 4) == 4 * i)).astype(BF16)
        total = total + mm(put, d_audio[pl.ds(i * half, half), :])
    d_slots[...] = total.astype(BF16)
    d_slots.send()
    attended = at[...].astype(F32).T.astype(BF16)
    for sink, blocks in ((to_core, (1, 3)), (keep, (0, 2))):
        for i, k in enumerate(blocks):
            part = mm(attended, group_block(wo.wait(), k, width))
            sink[pl.ds(i * rows, rows), :] = part.astype(BF16)
        sink.send()


def head_blocks(part_ref, extra, to_core, keep):
    rows = part_ref.shape[0]
    width = to_core.shape[1]
    me = lax.axis_index("head")
    for sink, blocks in ((to_core, (1, 3)), (keep, (0, 2))):
        for i, k in enumerate(blocks):
            cols = pl.ds(pl.multiple_of((me ^ k) * width, 128), width)
            sink[pl.ds(i * (rows + 16), rows), :] = part_ref[:, cols]
            sink[pl.ds(i * (rows + 16) + rows, 16), :] = extra
        sink.send()


def extra_rows(dots, width):
    row = to_row(jnp.sum(dots, axis=1, keepdims=True))
    row = jnp.concatenate((row, jnp.zeros((1, width - row.shape[1]), F32)), axis=1)
    return two_terms(row)


def video_project(dq, d_own, near, far, uq, u, weights, after, to_core, keep, part_ref):
    rows, width = uq.buf.shape
    queries = dq[...].astype(F32).T.astype(BF16)
    pair = (d_own[...].astype(F32) + near[...].astype(F32) + far[...].astype(F32)).astype(BF16)
    grads = (queries, pair[:rows], pair[rows:])
    others = (uq[...], u[pl.ds(0, rows), :], u[pl.ds(rows, rows), :])
    dots = sum(grad.astype(F32) * other.astype(F32) for grad, other in zip(grads, others))
    extra = extra_rows(dots, width)
    part = sum(mm(grad, weights.wait(i)[i], NT) for i, grad in enumerate(grads))
    part_ref[...] = part.astype(BF16)
    head_blocks(part_ref, extra, to_core, keep)


def sound_project(targets, back, sound_kv, audio_weights, to_core, keep, part_ref):
    rows = targets.buf.shape[1]
    width = to_core.shape[1]
    trow = targets[...]
    slot = slot_of(trow, to_col(trow), 1)
    arrived = back[...]
    slots = arrived.shape[0]
    grads = []
    for i in range(2):
        pick = (iota((rows, slots), 1) == slot + 4 * i).astype(BF16)
        grads.append(mm(pick, arrived).astype(BF16))
    others = (sound_kv[pl.ds(0, rows), :], sound_kv[pl.ds(rows, rows), :])
    dots = sum(grad.astype(F32) * other.astype(F32) for grad, other in zip(grads, others))
    extra = extra_rows(dots, width)
    part = sum(mm(grad, audio_weights.wait(i)[i], NT) for i, grad in enumerate(grads))
    part_ref[...] = part.astype(BF16)
    head_blocks(part_ref, extra, to_core, keep)


def pair_sum(*refs):
    cross, mine = refs[-2:]
    first = 0
    for keep, arrived in zip(refs[:-2:2], refs[1:-2:2]):
        tall = keep.buf.shape[0] // 2
        own, other = pl.ds(0, tall), pl.ds(tall, tall)
        block = pl.ds(first, tall)
        total = keep[other, :].astype(F32) + arrived[other, :].astype(F32)
        cross[block, :] = total.astype(BF16)
        if first + tall == mine.shape[0]:
            extra = total[tall - 16 : tall - 15] + total[tall - 15 : tall - 14]
            cross[pl.ds(first + tall - 16, 16), :] = two_terms(extra)
            cross.send()
        mine[block, :] = keep[own, :].astype(F32) + arrived[own, :].astype(F32)
        first += tall


def finish(tokens, audio, cotangent, scale_in, small, mine, cross, sound_mine, sound_cross,
           video_out, video_grad, audio_grad):
    rows, width = video_grad.shape
    sound_rows = audio_grad.shape[0]
    scale = scale_in[...][:, 0:1]

    def mean_of(total, count):
        row = (total[count : count + 1] + total[count + 1 : count + 2])[:, :count]
        return to_col(row * (1.0 / (4 * width)))

    inputs = tokens[...].astype(F32)
    normed = inputs * scale[:rows]
    video = mine[...] + cross[...].astype(F32)
    video_out[...] = (inputs + small[GATING : GATING + 1, :] * video[:rows]).astype(BF16)
    video_out.send()
    video = video[rows:]
    hat = video[:rows] * (1.0 + small[SCALES : SCALES + 1, :]) - normed * mean_of(video, rows)
    video_grad[...] = (cotangent[...].astype(F32) + scale[:rows] * hat).astype(BF16)
    video_grad.send()
    normed = audio[...].astype(F32) * scale[rows:]
    sound = sound_mine[...] + sound_cross[...].astype(F32)
    hat = sound[:sound_rows] - normed * mean_of(sound, sound_rows)
    audio_grad[...] = (scale[rows:] * hat).astype(BF16)


def per_device(
    video_tokens,
    cotangent,
    audio_frames,
    input_weights,
    audio_weights,
    output_weight,
    modulation,
    tile_clip,
    dropped,
    audio_tile,
):
    rows, model = video_tokens.shape
    width = input_weights.shape[2]
    sound_rows = audio_frames.shape[0]
    count = lax.axis_size("st")
    slots = 8 * count
    half = slots // 2
    pairs = width // 128
    targets = audio_tile.T
    modulation = jnp.transpose(modulation, (1, 0, 2))
    columns = [(slice(None), pl.ds(p * 128, 128)) for p in range(pairs)]
    head_rows = [(pl.ds(p * 128, 128), slice(None)) for p in range(pairs)]

    def layers(first, last):
        pieces = [(pl.ds(i, 1), pl.ds(i - first, 1)) for i in range(first, last)]
        return Taken((last - first, model, width), BF16, pieces)

    def own_block(n, dtype=BF16):
        return Taken((n, width), dtype, lambda: [((slice(None), my_columns(width)), slice(None))])

    def scalars(arg):
        return Taken(arg.shape, arg.dtype, space=pltpu.SMEM)

    def split(arg, pieces):
        return Taken(arg.shape, arg.dtype, [(piece, piece) for piece in pieces])

    kv, hidden, small, u, scale, sound_kv, sent = call(
        front,
        (scalars(tile_clip), scalars(dropped), None, None, layers(1, 3), None, None, layers(0, 2)),
        (tile_clip, dropped, modulation, video_tokens, input_weights, audio_frames, targets, audio_weights),
        [
            ((2 * rows, width), BF16),
            ((rows + 16, model), BF16),
            ((8, model), F32),
            ((2 * rows, width), BF16),
            ((rows + sound_rows, 128), F32),
            ((2 * sound_rows, width), BF16),
            ((slots, width), BF16),
        ],
        2 * (rows + sound_rows) * model * 2 * width,
        "front",
    )
    near_swap = [(i, i ^ 1) for i in range(count)]
    far_swap = [p for i in range(1, count - 2, 2) for p in ((i, i + 1), (i + 1, i))]
    near = lax.ppermute(kv, "st", near_swap)
    far = lax.ppermute(kv, "st", far_swap)
    arrived = lax.all_to_all(sent, "st", split_axis=0, concat_axis=0, tiled=True)
    block = ((rows, width), BF16)
    queries, uq, grads, grads_t = call(
        query_front,
        (None, layers(0, 1), None, None, None),
        (hidden, input_weights, cotangent, small, output_weight),
        [block, block, block, ((width, rows), BF16)],
        HEAVY,
        "query_front",
    )
    attended_t, dq_t, d_own, d_near, d_far, d_audio = call(
        attention,
        (None, split(arrived, columns), split(queries, columns), split(grads, columns))
        + (split(grads_t, head_rows),)
        + (split(kv, columns),) * 3,
        (small, arrived, queries, grads, grads_t, near, kv, far),
        [
            ((width, rows), BF16, head_rows),
            ((width, rows), BF16, head_rows),
            ((2 * rows, width), BF16, columns),
            ((2 * rows, width), BF16, columns),
            ((2 * rows, width), BF16, columns),
            ((slots, width), BF16, columns),
        ],
        2 * 6 * rows * (3 * rows + half) * width,
        "attention",
        (
            pltpu.VMEM((3 * rows + half, width), BF16),
            pltpu.VMEM((3 * rows + half, width), BF16),
            pltpu.VMEM((3 * rows + half, 128), F32),
        ),
    )
    back_near = lax.ppermute(d_near, "st", near_swap)
    back_far = lax.ppermute(d_far, "st", far_swap)
    groups = lax.axis_size("head")
    core_swap = [(i, i ^ 1) for i in range(groups)]
    cross_swap = [(i, i ^ 2) for i in range(groups)]
    two = ((2 * rows, width), BF16)
    d_slots, out_to_core, out_keep = call(
        out_first,
        (None, None, None),
        (d_audio, attended_t, output_weight),
        [((slots, width), BF16), two, two],
        HEAVY,
        "out_first",
    )
    back = lax.all_to_all(d_slots, "st", split_axis=0, concat_axis=0, tiled=True)
    out_from_core = lax.ppermute(out_to_core, "head", core_swap)

    def head_sum(body, ins, args, n, cost, name, before=(), above=0):
        both = ((2 * (n + 16), width), BF16)
        scratch = (pltpu.VMEM((n, model), BF16),)
        to_core, keep = call(body, ins, args, [both, both], cost, name, scratch)
        cross, mine = call(
            pair_sum,
            (None,) * (2 + len(before)),
            (*before, keep, lax.ppermute(to_core, "head", core_swap)),
            [((above + n + 16, width), BF16), ((above + n + 16, width), F32)],
            rows * width,
            name + "_sum",
        )
        return mine, lax.ppermute(cross, "head", cross_swap)

    video = head_sum(
        video_project,
        (None,) * 6 + (layers(0, 3), RAW),
        (dq_t, d_own, back_near, back_far, uq, u, input_weights, out_from_core),
        rows,
        HEAVY,
        "video",
        (out_keep, out_from_core),
        rows,
    )
    sound = head_sum(
        sound_project,
        (None,) * 3 + (layers(0, 2),),
        (targets, back, sound_kv, audio_weights),
        sound_rows,
        10**9,
        "sound",
    )
    return call(
        finish,
        (own_block(rows), own_block(sound_rows), own_block(rows), None, own_block(8, F32)) + (None,) * 4,
        (video_tokens, audio_frames, cotangent, scale, small, *video, *sound),
        [((rows, width), BF16), ((rows, width), BF16), ((sound_rows, width), BF16)],
        4 * rows * width,
        "finish",
    )


def solution(mesh):
    return jax.shard_map(
        per_device,
        mesh=mesh,
        in_specs=(
            P("st", None),
            P("st", None),
            P("st", None),
            P(None, None, "head"),
            P(None, None, "head"),
            P("head", None),
            P(),
            P(),
            P(),
            P("st", None),
        ),
        out_specs=(P("st", "head"), P("st", "head"), P("st", "head")),
        check_vma=False,
    )
```

```python
import jax
import jax.numpy as jnp
from jax import lax
from jax.experimental import pallas as pl
from jax.experimental.pallas import tpu as pltpu
from jax.sharding import PartitionSpec as P

HD = 64
EPS = 1e-06
DEAD = -1e30
EMPTY = 32768.0
LOG4 = 1.3862943611198906
F32 = jnp.float32
BF16 = jnp.bfloat16
VMEM_LIMIT = 60 * 1024 * 1024
HEAVY = 10**13

NN = (((1,), (0,)), ((), ()))
NT = (((1,), (1,)), ((), ()))
TN = (((0,), (0,)), ((), ()))


def mm(a, b, dims=NN):
    return lax.dot_general(a, b, dims, preferred_element_type=F32)


def iota(shape, dim):
    return lax.broadcasted_iota(jnp.int32, shape, dim)


def row_scale(matrix):
    return lax.rsqrt(jnp.mean(matrix * matrix, axis=-1, keepdims=True) + EPS)


def to_row(col):
    n = col.shape[0]
    eye = iota((n, n), 0) == iota((n, n), 1)
    return jnp.sum(jnp.where(eye, col, jnp.zeros_like(col)), axis=0, keepdims=True)


def to_col(row):
    n = row.shape[1]
    eye = iota((n, n), 0) == iota((n, n), 1)
    return jnp.sum(jnp.where(eye, row, jnp.zeros_like(row)), axis=1, keepdims=True)


class Source:
    def __init__(self, ref, buf, sems, first, pieces):
        self.buf = buf
        self.copies = []
        self.done = []
        for i, piece in enumerate(pieces):
            src, dst = (ref, buf) if piece is None else (ref.at[piece[0]], buf.at[piece[1]])
            self.copies.append(pltpu.make_async_copy(src, dst, sems.at[first + i]))
            self.done.append(False)

    def start(self, i):
        self.copies[i].start()

    def wait(self, i=0):
        if not self.done[i]:
            self.done[i] = True
            self.copies[i].wait()
        return self.buf

    def __getitem__(self, at):
        return self.wait()[at]


class Sink:
    def __init__(self, ref, buf, sems, first, pieces):
        self.buf = buf
        self.shape = buf.shape
        self.dtype = buf.dtype
        self.copies = []
        self.started = []
        for i, piece in enumerate(pieces):
            src, dst = (buf, ref) if piece is None else (buf.at[piece], ref.at[piece])
            self.copies.append(pltpu.make_async_copy(src, dst, sems.at[first + i]))
            self.started.append(False)

    def __setitem__(self, at, value):
        self.buf[at] = value

    def send(self, i=0):
        if not self.started[i]:
            self.started[i] = True
            self.copies[i].start()


class Taken:
    def __init__(self, shape, dtype, pieces=(None,), space=pltpu.VMEM):
        self.shape, self.dtype, self.pieces, self.space = shape, dtype, pieces, space
        self.count = 1 if callable(pieces) else len(pieces)


RAW = "raw"
HBM = pl.BlockSpec(memory_space=pl.ANY)


def call(body, ins, args, outs, flops, name, scratch=()):
    specs = [Taken(arg.shape, arg.dtype) if spec is None else spec for spec, arg in zip(ins, args)]
    taken = [spec for spec in specs if isinstance(spec, Taken)]
    outs = [out if len(out) == 3 else out + ((None,),) for out in outs]
    n_in = sum(spec.count for spec in taken)
    n_out = sum(len(pieces) for _, _, pieces in outs)

    def kernel(*refs):
        in_refs = refs[: len(specs)]
        out_refs = refs[len(specs) : len(specs) + len(outs)]
        rest = refs[len(specs) + len(outs) :]
        in_bufs = rest[: len(taken)]
        out_bufs = rest[len(taken) : len(taken) + len(outs)]
        in_sems, out_sems = rest[len(taken) + len(outs) : len(taken) + len(outs) + 2]
        extra = rest[len(taken) + len(outs) + 2 :]
        operands, sources, first = [], [], 0
        for spec, ref in zip(specs, in_refs):
            if not isinstance(spec, Taken):
                operands.append(ref)
                continue
            pieces = spec.pieces() if callable(spec.pieces) else spec.pieces
            source = Source(ref, in_bufs[len(sources)], in_sems, first, pieces)
            operands.append(source)
            sources.append(source)
            first += spec.count
        for i in range(max(spec.count for spec in taken)):
            for source in sources:
                if i < len(source.copies):
                    source.start(i)
        sinks, first = [], 0
        for (_, _, pieces), ref, buf in zip(outs, out_refs, out_bufs):
            sinks.append(Sink(ref, buf, out_sems, first, pieces))
            first += len(pieces)
        body(*operands, *sinks, *extra)
        for sink in sinks:
            for i in range(len(sink.copies)):
                sink.send(i)
        for source in sources:
            for i in range(len(source.copies)):
                source.wait(i)
        for sink in sinks:
            for copy in sink.copies:
                copy.wait()

    return pl.pallas_call(
        kernel,
        in_specs=[HBM] * len(specs),
        out_specs=[HBM] * len(outs),
        out_shape=[jax.ShapeDtypeStruct(shape, dtype) for shape, dtype, _ in outs],
        scratch_shapes=[spec.space(spec.shape, spec.dtype) for spec in taken]
        + [pltpu.VMEM(shape, dtype) for shape, dtype, _ in outs]
        + [pltpu.SemaphoreType.DMA((n_in,)), pltpu.SemaphoreType.DMA((n_out,))]
        + list(scratch),
        compiler_params=pltpu.CompilerParams(vmem_limit_bytes=VMEM_LIMIT),
        cost_estimate=pl.CostEstimate(flops=flops, bytes_accessed=4 << 20, transcendentals=0),
        name=name,
    )(*args)


def my_columns(width):
    return pl.ds(pl.multiple_of(lax.axis_index("head") * width, 128), width)


def two_terms(row):
    high = row.astype(BF16).astype(F32)
    where_row = iota((16, row.shape[1]), 0)
    return jnp.where(where_row == 0, high, jnp.where(where_row == 1, row - high, 0.0)).astype(BF16)


def slot_of(trow, tcol, axis):
    n = trow.shape[1]
    earlier = (tcol == trow) & (iota((n, n), axis) < iota((n, n), 1 - axis))
    rank = jnp.sum(earlier.astype(jnp.int32), axis=axis, keepdims=True)
    return (trow if axis == 0 else tcol) * 8 + rank


SHIFTS, SCALES, GATING, NEAR, FAR, SOUND = range(6)


def video_front(clips, drops, mod, tokens, weights, kv, hidden, small, u, scale_out):
    rows = tokens.buf.shape[0]
    position = lax.axis_index("st")
    count = clips.buf.shape[0]
    clip_ref, dropped_ref = clips.wait(), drops.wait()
    clip = clip_ref[position]
    odd = position & 1

    def side_bias(tile):
        inside = (tile >= 0) & (tile < count)
        other = clip_ref[jnp.clip(tile, 0, count - 1)]
        return jnp.where(inside & (other == clip), -LOG4, DEAD)

    near = side_bias(position + 1 - 2 * odd)
    far = side_bias(position - 1 + 2 * odd)
    sound = jnp.where(dropped_ref[clip] == 0, -LOG4, DEAD)
    shifts, scales, gating = [mod[i, pl.ds(clip, 1), :] for i in range(3)]
    at = iota((8, shifts.shape[1]), 0)
    table = jnp.where(at == SHIFTS, shifts, jnp.where(at == SCALES, scales, gating))
    table = jnp.where(at == NEAR, near, jnp.where(at == FAR, far, table))
    small[...] = jnp.where(at == SOUND, sound, table)
    small.send()
    inputs = tokens[...].astype(F32)
    scale = row_scale(inputs)
    both = jnp.concatenate(
        ((inputs * scale * (1.0 + scales) + shifts).astype(BF16), two_terms(shifts)), axis=0
    )
    for i in range(2):
        block = pl.ds(i * rows, rows)
        made = mm(both, weights.wait(i)[i])
        kv[block, :] = made[:rows].astype(BF16)
        u[block, :] = (made[:rows] - (made[rows : rows + 1] + made[rows + 1 : rows + 2])).astype(BF16)
    kv.send()
    u.send()
    hidden[...] = both
    hidden.send()
    scale_out[...] = jnp.broadcast_to(scale, (rows, 128))


def sound_front(audio, targets, audio_weights, after, scale_out, sound_kv, sent):
    sound_rows = audio.buf.shape[0]
    sounds = audio[...].astype(F32)
    sound_scale = row_scale(sounds)
    scale_out[...] = jnp.broadcast_to(sound_scale, (sound_rows, 128))
    scale_out.send()
    sound_in = (sounds * sound_scale).astype(BF16)
    trow = targets[...]
    slot = slot_of(trow, to_col(trow), 0)
    slots = sent.shape[0]
    place = iota((slots, sound_rows), 0)
    dispatch = jnp.concatenate((place == slot, place == slot + 4), axis=1).astype(BF16)
    filled = jnp.sum(dispatch.astype(F32), axis=1, keepdims=True)
    pairs = [mm(sound_in, audio_weights.wait(i)[i]).astype(BF16) for i in range(2)]
    pairs = jnp.concatenate(pairs, axis=0)
    sound_kv[...] = pairs
    sound_kv.send()
    made = mm(dispatch, pairs)
    mark = ((iota(made.shape, 0) & 7) < 4) & (iota(made.shape, 1) == 0) & (filled < 0.5)
    sent[...] = jnp.where(mark, EMPTY, made).astype(BF16)


def query_front(hidden, wq, cotangent, small, wo, q, uq, g, gt):
    rows = q.shape[0]
    made = mm(hidden[...], wq[0])
    queries = made[:rows].astype(BF16)
    q[...] = (queries.astype(F32) * (float(HD) ** -0.5)).astype(BF16)
    q.send()
    uq[...] = (made[:rows] - (made[rows : rows + 1] + made[rows + 1 : rows + 2])).astype(BF16)
    uq.send()
    out_grad = (cotangent[...].astype(F32) * small[GATING : GATING + 1, :]).astype(BF16)
    grads = mm(out_grad, wo[...], NT)
    g[...] = grads.astype(BF16)
    g.send()
    gt[...] = grads.T.astype(BF16)


def attention(small, slots_in, q_in, g_in, gt_in, near, own, far,
              at, dq, d_own, d_near, d_far, d_audio, k_all, v_all, bias_ref):
    rows, width = q_in.buf.shape
    slots = slots_in.buf.shape[0]
    half = slots // 2
    table = small[:, 0:128]
    for i, bias in enumerate((table[NEAR : NEAR + 1], None, table[FAR : FAR + 1])):
        bias = jnp.full((1, 128), -LOG4, F32) if bias is None else bias
        bias_ref[pl.ds(i * rows, rows), :] = jnp.broadcast_to(bias, (rows, 128))
    pick_at = (iota((half, slots), 0) >> 2) * 8 + (iota((half, slots), 0) & 3)
    picks = [(iota((half, slots), 1) == pick_at + 4 * i).astype(BF16) for i in range(2)]
    lane = iota((rows, 128), 1)
    sinks = (d_near, d_own, d_far)
    tail = pl.ds(3 * rows, half)
    saved = []
    for pair in range(width // 128):
        cols = slice(pair * 128, (pair + 1) * 128)
        arrived = slots_in.wait(pair)[:, cols]
        k_all[tail, cols] = mm(picks[0], arrived).astype(BF16)
        v_all[tail, cols] = mm(picks[1], arrived).astype(BF16)
        if pair == 0:
            live = k_all[tail, cols].astype(F32)[:, 0:1] < EMPTY * 0.5
            sound = jnp.broadcast_to(table[SOUND : SOUND + 1], (half, 128))
            bias_ref[tail, :] = jnp.where(live, sound, DEAD)
        q_pair = q_in.wait(pair)[:, cols]
        g_pair = g_in.wait(pair)[:, cols]
        gt_pair = gt_in.wait(pair)[cols, :]
        for i, source in enumerate((near, own, far)):
            block = pl.ds(i * rows, rows)
            got = source.wait(pair)
            k_all[block, cols] = got[pl.ds(0, rows), cols]
            v_all[block, cols] = got[pl.ds(rows, rows), cols]
        keys = k_all[:, cols]
        values = v_all[:, cols]
        keys_t = keys.T
        values_t = values.T
        qs, gs, ps, ss = [], [], [], []
        bias = jnp.concatenate([bias_ref[...]] * 2, axis=1)
        for side in range(2):
            mine = (lane // HD) == side
            qs.append(jnp.where(mine, q_pair, jnp.zeros_like(q_pair)))
            gs.append(jnp.where(mine, g_pair, jnp.zeros_like(g_pair)))
        scores = mm(keys, jnp.concatenate(qs, axis=0), NT)
        scores = [scores[:, :rows], scores[:, rows:]]
        grads = mm(values, jnp.concatenate(gs, axis=0), NT)
        grads = [grads[:, :rows], grads[:, rows:]]
        probs = []
        for side in range(2):
            weights = jnp.exp(scores[side] + bias)
            probs.append(weights * (1.0 / jnp.sum(weights, axis=0, keepdims=True)))
            ps.append(probs[side].astype(BF16))
        atts = [mm(values_t[i * HD : (i + 1) * HD], ps[i]).astype(BF16) for i in range(2)]
        saved.append((cols, keys, values, keys_t, qs, gs, ps, ss, probs, grads, atts, gt_pair))
    for pair, (cols, keys, values, keys_t, qs, gs, ps, ss, probs, grads, atts, gt_pair) in enumerate(saved):
        for side in range(2):
            half_rows = slice(side * HD, (side + 1) * HD)
            head_rows = slice(pair * 128 + side * HD, pair * 128 + (side + 1) * HD)
            at[head_rows, :] = atts[side]
            dots = jnp.sum(atts[side].astype(F32) * gt_pair[half_rows].astype(F32), axis=0, keepdims=True)
            ss.append((probs[side] * (grads[side] - dots)).astype(BF16))
        for side in range(2):
            half_rows = slice(side * HD, (side + 1) * HD)
            head_rows = slice(pair * 128 + side * HD, pair * 128 + (side + 1) * HD)
            dqs = mm(keys_t[half_rows], ss[side]) * (float(HD) ** -0.5)
            dq[head_rows, :] = dqs.astype(BF16)
        d_keys = mm(jnp.concatenate(ss, axis=1), jnp.concatenate(qs, axis=0))
        d_values = mm(jnp.concatenate(ps, axis=1), jnp.concatenate(gs, axis=0))
        for b, sink in enumerate(sinks):
            block = slice(b * rows, (b + 1) * rows)
            sink[pl.ds(0, rows), cols] = d_keys[block].astype(sink.dtype)
            sink[pl.ds(rows, rows), cols] = d_values[block].astype(sink.dtype)
        d_audio[pl.ds(0, half), cols] = d_keys[3 * rows :].astype(BF16)
        d_audio[pl.ds(half, half), cols] = d_values[3 * rows :].astype(BF16)
        for sink in (at, dq, d_own, d_near, d_far, d_audio):
            sink.send(pair)


def group_block(weights, k, width):
    return weights[:, pl.ds(pl.multiple_of((lax.axis_index("head") ^ k) * width, 128), width)]


def out_first(d_audio, at, wo, d_slots, to_core, keep):
    slots, width = d_slots.shape
    half = slots // 2
    rows = at.buf.shape[1]
    back_row = iota((slots, half), 0)
    back_at = (back_row >> 3) * 4 + (back_row & 3)
    total = jnp.zeros((slots, width), F32)
    for i in range(2):
        put = ((iota((slots, half), 1) == back_at) & ((back_row & 4) == 4 * i)).astype(BF16)
        total = total + mm(put, d_audio[pl.ds(i * half, half), :])
    d_slots[...] = total.astype(BF16)
    d_slots.send()
    attended = at[...].astype(F32).T.astype(BF16)
    for sink, blocks in ((to_core, (1, 3)), (keep, (0, 2))):
        for i, k in enumerate(blocks):
            part = mm(attended, group_block(wo.wait(), k, width))
            sink[pl.ds(i * rows, rows), :] = part.astype(BF16)
        sink.send()


def head_blocks(part_ref, extra, to_core, keep):
    rows = part_ref.shape[0]
    width = to_core.shape[1]
    me = lax.axis_index("head")
    for sink, blocks in ((to_core, (1, 3)), (keep, (0, 2))):
        for i, k in enumerate(blocks):
            cols = pl.ds(pl.multiple_of((me ^ k) * width, 128), width)
            sink[pl.ds(i * (rows + 16), rows), :] = part_ref[:, cols]
            sink[pl.ds(i * (rows + 16) + rows, 16), :] = extra
        sink.send()


def extra_rows(dots, width):
    row = to_row(jnp.sum(dots, axis=1, keepdims=True))
    row = jnp.concatenate((row, jnp.zeros((1, width - row.shape[1]), F32)), axis=1)
    return two_terms(row)


def video_project(dq, d_own, near, far, uq, u, weights, after, to_core, keep, part_ref):
    rows, width = uq.buf.shape
    queries = dq[...].astype(F32).T.astype(BF16)
    pair = (d_own[...].astype(F32) + near[...].astype(F32) + far[...].astype(F32)).astype(BF16)
    grads = (queries, pair[:rows], pair[rows:])
    others = (uq[...], u[pl.ds(0, rows), :], u[pl.ds(rows, rows), :])
    dots = sum(grad.astype(F32) * other.astype(F32) for grad, other in zip(grads, others))
    extra = extra_rows(dots, width)
    part = sum(mm(grad, weights.wait(i)[i], NT) for i, grad in enumerate(grads))
    part_ref[...] = part.astype(BF16)
    head_blocks(part_ref, extra, to_core, keep)


def sound_project(targets, back, sound_kv, audio_weights, to_core, keep, part_ref):
    rows = targets.buf.shape[1]
    width = to_core.shape[1]
    trow = targets[...]
    slot = slot_of(trow, to_col(trow), 1)
    arrived = back[...]
    slots = arrived.shape[0]
    grads = []
    for i in range(2):
        pick = (iota((rows, slots), 1) == slot + 4 * i).astype(BF16)
        grads.append(mm(pick, arrived).astype(BF16))
    others = (sound_kv[pl.ds(0, rows), :], sound_kv[pl.ds(rows, rows), :])
    dots = sum(grad.astype(F32) * other.astype(F32) for grad, other in zip(grads, others))
    extra = extra_rows(dots, width)
    part = sum(mm(grad, audio_weights.wait(i)[i], NT) for i, grad in enumerate(grads))
    part_ref[...] = part.astype(BF16)
    head_blocks(part_ref, extra, to_core, keep)


def pair_sum(*refs):
    cross, mine = refs[-2:]
    first = 0
    for keep, arrived in zip(refs[:-2:2], refs[1:-2:2]):
        tall = keep.buf.shape[0] // 2
        own, other = pl.ds(0, tall), pl.ds(tall, tall)
        block = pl.ds(first, tall)
        total = keep[other, :].astype(F32) + arrived[other, :].astype(F32)
        cross[block, :] = total.astype(BF16)
        if first + tall == mine.shape[0]:
            extra = total[tall - 16 : tall - 15] + total[tall - 15 : tall - 14]
            cross[pl.ds(first + tall - 16, 16), :] = two_terms(extra)
            cross.send()
        mine[block, :] = keep[own, :].astype(F32) + arrived[own, :].astype(F32)
        first += tall


def mean_of(total, count):
    row = (total[count : count + 1] + total[count + 1 : count + 2])[:, :count]
    return to_col(row * (1.0 / (4 * total.shape[1])))


def finish_video(tokens, cotangent, scale_in, small, mine, cross, video_out, video_grad):
    rows = video_grad.shape[0]
    scale = scale_in[...][:, 0:1]
    inputs = tokens[...].astype(F32)
    video = mine[...] + cross[...].astype(F32)
    video_out[...] = (inputs + small[GATING : GATING + 1, :] * video[:rows]).astype(BF16)
    video_out.send()
    video = video[rows:]
    hat = video[:rows] * (1.0 + small[SCALES : SCALES + 1, :]) - inputs * scale * mean_of(video, rows)
    video_grad[...] = (cotangent[...].astype(F32) + scale * hat).astype(BF16)


def finish_sound(audio, scale_in, mine, cross, after, audio_grad):
    rows = audio_grad.shape[0]
    scale = scale_in[...][:, 0:1]
    normed = audio[...].astype(F32) * scale
    sound = mine[...] + cross[...].astype(F32)
    audio_grad[...] = (scale * (sound[:rows] - normed * mean_of(sound, rows))).astype(BF16)


def per_device(
    video_tokens,
    cotangent,
    audio_frames,
    input_weights,
    audio_weights,
    output_weight,
    modulation,
    tile_clip,
    dropped,
    audio_tile,
):
    rows, model = video_tokens.shape
    width = input_weights.shape[2]
    sound_rows = audio_frames.shape[0]
    count = lax.axis_size("st")
    slots = 8 * count
    half = slots // 2
    pairs = width // 128
    targets = audio_tile.T
    modulation = jnp.transpose(modulation, (1, 0, 2))
    columns = [(slice(None), pl.ds(p * 128, 128)) for p in range(pairs)]
    head_rows = [(pl.ds(p * 128, 128), slice(None)) for p in range(pairs)]

    def layers(first, last):
        pieces = [(pl.ds(i, 1), pl.ds(i - first, 1)) for i in range(first, last)]
        return Taken((last - first, model, width), BF16, pieces)

    def own_block(n, dtype=BF16):
        return Taken((n, width), dtype, lambda: [((slice(None), my_columns(width)), slice(None))])

    def scalars(arg):
        return Taken(arg.shape, arg.dtype, space=pltpu.SMEM)

    def split(arg, pieces):
        return Taken(arg.shape, arg.dtype, [(piece, piece) for piece in pieces])

    kv, hidden, small, u, scale = call(
        video_front,
        (scalars(tile_clip), scalars(dropped), None, None, layers(1, 3)),
        (tile_clip, dropped, modulation, video_tokens, input_weights),
        [
            ((2 * rows, width), BF16),
            ((rows + 16, model), BF16),
            ((8, model), F32),
            ((2 * rows, width), BF16),
            ((rows, 128), F32),
        ],
        2 * rows * model * 2 * width,
        "video_front",
    )
    sound_scale, sound_kv, sent = call(
        sound_front,
        (None, None, layers(0, 2), RAW),
        (audio_frames, targets, audio_weights, kv),
        [((sound_rows, 128), F32), ((2 * sound_rows, width), BF16), ((slots, width), BF16)],
        2 * sound_rows * model * 2 * width,
        "sound_front",
    )
    near_swap = [(i, i ^ 1) for i in range(count)]
    far_swap = [p for i in range(1, count - 2, 2) for p in ((i, i + 1), (i + 1, i))]
    near = lax.ppermute(kv, "st", near_swap)
    far = lax.ppermute(kv, "st", far_swap)
    arrived = lax.all_to_all(sent, "st", split_axis=0, concat_axis=0, tiled=True)
    block = ((rows, width), BF16)
    queries, uq, grads, grads_t = call(
        query_front,
        (None, layers(0, 1), None, None, None),
        (hidden, input_weights, cotangent, small, output_weight),
        [block, block, block, ((width, rows), BF16)],
        HEAVY,
        "query_front",
    )
    attended_t, dq_t, d_own, d_near, d_far, d_audio = call(
        attention,
        (None, split(arrived, columns), split(queries, columns), split(grads, columns))
        + (split(grads_t, head_rows),)
        + (split(kv, columns),) * 3,
        (small, arrived, queries, grads, grads_t, near, kv, far),
        [
            ((width, rows), BF16, head_rows),
            ((width, rows), BF16, head_rows),
            ((2 * rows, width), BF16, columns),
            ((2 * rows, width), BF16, columns),
            ((2 * rows, width), BF16, columns),
            ((slots, width), BF16, columns),
        ],
        2 * 6 * rows * (3 * rows + half) * width,
        "attention",
        (
            pltpu.VMEM((3 * rows + half, width), BF16),
            pltpu.VMEM((3 * rows + half, width), BF16),
            pltpu.VMEM((3 * rows + half, 128), F32),
        ),
    )
    back_near = lax.ppermute(d_near, "st", near_swap)
    back_far = lax.ppermute(d_far, "st", far_swap)
    groups = lax.axis_size("head")
    core_swap = [(i, i ^ 1) for i in range(groups)]
    cross_swap = [(i, i ^ 2) for i in range(groups)]
    two = ((2 * rows, width), BF16)
    d_slots, out_to_core, out_keep = call(
        out_first,
        (None, None, None),
        (d_audio, attended_t, output_weight),
        [((slots, width), BF16), two, two],
        HEAVY,
        "out_first",
    )
    back = lax.all_to_all(d_slots, "st", split_axis=0, concat_axis=0, tiled=True)
    out_from_core = lax.ppermute(out_to_core, "head", core_swap)

    def head_sum(body, ins, args, n, cost, name, before=(), above=0):
        both = ((2 * (n + 16), width), BF16)
        scratch = (pltpu.VMEM((n, model), BF16),)
        to_core, keep = call(body, ins, args, [both, both], cost, name, scratch)
        cross, mine = call(
            pair_sum,
            (None,) * (2 + len(before)),
            (*before, keep, lax.ppermute(to_core, "head", core_swap)),
            [((above + n + 16, width), BF16), ((above + n + 16, width), F32)],
            rows * width,
            name + "_sum",
        )
        return mine, lax.ppermute(cross, "head", cross_swap)

    video = head_sum(
        video_project,
        (None,) * 6 + (layers(0, 3), RAW),
        (dq_t, d_own, back_near, back_far, uq, u, input_weights, out_from_core),
        rows,
        HEAVY,
        "video",
        (out_keep, out_from_core),
        rows,
    )
    sound = head_sum(
        sound_project,
        (None,) * 3 + (layers(0, 2),),
        (targets, back, sound_kv, audio_weights),
        sound_rows,
        10**9,
        "sound",
    )
    video_out, video_grad = call(
        finish_video,
        (own_block(rows), own_block(rows), None, own_block(8, F32), None, None),
        (video_tokens, cotangent, scale, small, *video),
        [((rows, width), BF16), ((rows, width), BF16)],
        4 * rows * width,
        "finish_video",
    )
    (audio_grad,) = call(
        finish_sound,
        (own_block(sound_rows), None, None, None, RAW),
        (audio_frames, sound_scale, *sound, video_grad),
        [((sound_rows, width), BF16)],
        2 * sound_rows * width,
        "finish_sound",
    )
    return video_out, video_grad, audio_grad


def solution(mesh):
    return jax.shard_map(
        per_device,
        mesh=mesh,
        in_specs=(
            P("st", None),
            P("st", None),
            P("st", None),
            P(None, None, "head"),
            P(None, None, "head"),
            P("head", None),
            P(),
            P(),
            P(),
            P("st", None),
        ),
        out_specs=(P("st", "head"), P("st", "head"), P("st", "head")),
        check_vma=False,
    )
```
